512 devices in a mesh: seq: 64 (over y, x, core), tp: 8 (over z).
Axes of the slice: x: 4, y: 8, z: 8, core: 2. Of those that a mesh axis runs over, the one named last changes fastest.
Arguments:
- tokens: bfloat16 [16384, 4096], P('seq', 'tp'), may hold values from -30 to 30
- w_qkv: bfloat16 [4096, 3, 2048], P('seq', None, 'tp'), may hold values from -1 to 1
- keep_list: int32 [8192], P('seq'), may hold values from 0 to 255, as said below
- counts: int32 [64], P('seq'), may hold values from 1 to 127, as said below
Outputs:
- attended: bfloat16 [4096, 2048], P('seq', 'tp')
The draws below stay inside these ranges and needn't reach their ends.
Inputs may be any that keep to these rules, and one draw needn't show every extreme that they name: `counts`: the entries sum to 4096; one shard keeps 2 * 64 - 1 tokens and one shard keeps 1. `keep_list`: entries s * 2 * 64 to s * 2 * 64 + 2 * 64 - 1 are distinct token indices within shard s; the first counts[s] of them increase.
All inputs are finite; a program needn't handle non-finite values.
Results may differ from the reference program's by a relative error of at most 0.0065.
Values may be sent and summed in bfloat16 or wider, within the bound.
A program may use at most 64 MiB of HBM per device.

```python
import jax
import jax.numpy as jnp
from jax import lax

D = 4096
HEADS = 16
HD = 128
TOK_DEV = 256
CAP = 64
TOKENS = 16384
KEPT = 4096


def keep_plan(key):
    shards = KEPT // CAP
    base = jax.random.fold_in(key, 11)
    pick_key, shift_key, perm_key = jax.random.split(base, 3)
    order = jax.random.permutation(pick_key, shards)
    shift = jax.random.randint(shift_key, (shards // 2,), 0, CAP).astype(jnp.int32)
    shift = shift.at[0].set(CAP - 1)
    counts = jnp.zeros((shards,), jnp.int32)
    counts = counts.at[order[:shards // 2]].set(CAP + shift)
    counts = counts.at[order[shards // 2:]].set(CAP - shift)
    row_keys = jax.random.split(perm_key, shards)
    chosen = jax.vmap(lambda single: jax.random.permutation(single, TOK_DEV)[:2 * CAP])(row_keys)
    slot_ids = jnp.arange(2 * CAP, dtype=jnp.int32)
    ranked = jnp.where(slot_ids[None, :] < counts[:, None], chosen, chosen + TOK_DEV)
    keep = jnp.sort(ranked, axis=1) % TOK_DEV
    return (counts, keep.reshape(-1).astype(jnp.int32))


def draw_counts(key, part):
    return keep_plan(key)[0]


def draw_keep_list(key, part):
    return keep_plan(key)[1]


def draw_tokens(key, part):
    first_key = jax.random.fold_in(key, 0)
    values = jax.random.normal(first_key, (TOKENS, D), jnp.float32)
    return jnp.clip(values, -6.0, 6.0).astype(jnp.bfloat16)


def draw_w_qkv(key, part):
    values = jax.random.normal(key, (D, 3, HEADS * HD), jnp.float32) * D ** (-0.5)
    return jnp.clip(values, -1.0, 1.0).astype(jnp.bfloat16)


def setup_inputs(seed: int = 0) -> dict:
    seeds = jax.random.split(jax.random.key(seed), 5)
    return {
        "tokens": draw_tokens(jax.random.fold_in(seeds[4], 71), 0),
        "w_qkv": draw_w_qkv(jax.random.fold_in(seeds[4], 71), 0),
        "keep_list": draw_keep_list(jax.random.fold_in(seeds[4], 71), 0),
        "counts": draw_counts(jax.random.fold_in(seeds[4], 71), 0),
    }


def reference(tokens, w_qkv, keep_list, counts):
    shards = counts.shape[0]
    tok_dev = tokens.shape[0] // shards
    slots = keep_list.shape[0] // shards
    kept_total = shards * CAP
    ends = jnp.cumsum(counts).astype(jnp.int32)
    starts = (ends - counts).astype(jnp.int32)
    rows = jnp.arange(kept_total, dtype=jnp.int32)
    ranks = (rows % CAP) * shards + rows // CAP
    source = jnp.sum((ends[None, :] <= ranks[:, None]).astype(jnp.int32), axis=1).astype(jnp.int32)
    within = ranks - starts[source]
    local = keep_list[source * slots + within]
    positions = (source * tok_dev + local).astype(jnp.int32)
    chosen = tokens[positions]
    projected = jnp.dot(chosen, w_qkv.reshape(D, 3 * HEADS * HD), preferred_element_type=jnp.float32)
    projected = projected.astype(jnp.bfloat16).reshape(kept_total, 3, HEADS, HD)
    heads_first = jnp.transpose(projected, (2, 1, 0, 3))
    causal = positions[None, :] > positions[:, None]

    def one_head(block):
        scores = jnp.dot(block[0], block[1].T, preferred_element_type=jnp.float32) * (HD ** -0.5)
        scores = jnp.where(causal, -jnp.inf, scores)
        top = jnp.max(scores, axis=1, keepdims=True)
        expo = jnp.exp(scores - top)
        weights = expo.astype(jnp.bfloat16)
        numer = jnp.dot(weights, block[2], preferred_element_type=jnp.float32)
        return numer / jnp.sum(expo, axis=1)[:, None]

    outputs = lax.map(one_head, heads_first)
    return jnp.transpose(outputs, (1, 0, 2)).reshape(kept_total, HEADS * HD).astype(jnp.bfloat16)
```

```python
import math

import jax
import jax.numpy as jnp
from jax import lax
from jax.experimental import pallas as pl
from jax.experimental.pallas import tpu as pltpu
from jax.sharding import PartitionSpec as P

MESH = pl.DeviceIdType.MESH
NX, NY, NZ = 4, 8, 8
HD = 128
BF = jnp.bfloat16
F32 = jnp.float32
SEMS = 220


class Links:
    def __init__(self, send_sem, recv_sem):
        self.send_sem, self.recv_sem, self.count, self.copies = send_sem, recv_sem, 0, []

    def send(self, src, dst, device):
        copy = pltpu.make_async_remote_copy(
            src_ref=src,
            dst_ref=dst,
            send_sem=self.send_sem.at[self.count],
            recv_sem=self.recv_sem.at[self.count],
            device_id=device,
            device_id_type=MESH,
        )
        self.count += 1
        copy.start()
        self.copies.append(copy)
        return copy

    def drain(self):
        for copy in self.copies:
            copy.wait_send()


class Gather:
    def __init__(self, links, buf, place):
        self.links, self.buf = links, buf
        self.x, self.y, self.dev = place
        self.xp, self.xm, self.x2 = [(self.x + k) % NX for k in (1, 3, 2)]

    def row(self, k):
        return (self.y + k + NY) % NY

    def put(self, y, x, rows, to):
        lo, hi = rows
        piece = self.buf.at[y, pl.ds(0, NX) if x is None else x, pl.ds(lo, hi - lo)]
        ty, tx = to
        return self.links.send(piece, piece, self.dev(ty, tx))

    def along_x(self, y, x, rows):
        return (self.put(y, x, rows, (self.y, self.xp)), self.put(y, x, rows, (self.y, self.xm)))

    def steps(self):
        one, two = (0, 48), (48, 128)
        one_a, one_b, two_a, two_b = (0, 32), (32, 48), (48, 96), (96, 128)
        x, y, xp, xm, x2 = self.x, self.y, self.xp, self.xm, self.x2
        up, down = (self.row(1), x), (self.row(-1), x)

        def arrive(copies):
            for copy in copies:
                copy.wait_recv()

        def both_y(chunk, rows):
            return [self.put(y, chunk, rows, up), self.put(y, chunk, rows, down)]

        def on_y(k, chunk, rows_a, rows_b):
            return [
                self.put(self.row(1 - k), chunk, rows_a, up),
                self.put(self.row(k - 1), chunk, rows_b, down),
            ]

        def on_x(rows_list):
            done = []
            for r in rows_list:
                done += self.along_x(r, x, two)
            return done

        def half_x(rows_list):
            done = []
            for r in rows_list:
                done.append(self.put(r, xm, two_a, (y, xp)))
                done.append(self.put(r, xp, two_b, (y, xm)))
            return done

        first = self.along_x(y, x, one)
        ys = {1: on_y(1, x, two, two)}
        xs = {0: on_x([y])}
        tall = {1: both_y(x, one)}
        late = []
        yield
        arrive(ys[1])
        ys[2] = on_y(2, x, two, two)
        xs[1] = on_x([self.row(-1), self.row(1)])
        yield
        arrive(first)
        half = [self.put(y, xm, one_a, (y, xp)), self.put(y, xp, one_b, (y, xm))]
        tall[1] += both_y(xm, one) + both_y(xp, one)
        yield
        arrive(xs[0])
        late += half_x([y])
        yield
        arrive(ys[2])
        ys[3] = on_y(3, x, two, two)
        xs[2] = on_x([self.row(-2), self.row(2)])
        yield
        arrive(half)
        tall[1] += both_y(x2, one)
        yield
        arrive(tall[1])
        tall[2] = on_y(2, None, one, one)
        yield
        arrive(ys[3])
        ys[4] = on_y(4, x, two_a, two_b)
        xs[3] = on_x([self.row(-3), self.row(3)])
        yield
        arrive(xs[1])
        late += half_x([self.row(-1), self.row(1)])
        yield
        arrive(ys[4])
        xs[4] = on_x([self.row(4)])
        yield
        arrive(tall[2])
        tall[3] = on_y(3, None, one, one)
        yield
        arrive(xs[2])
        late += half_x([self.row(-2), self.row(2)])
        yield
        arrive(tall[3])
        tall[4] = on_y(4, None, one_a, one_b)
        yield
        arrive(xs[3])
        late += half_x([self.row(-3), self.row(3)])
        yield
        arrive(xs[4])
        late += half_x([self.row(4)])
        yield
        arrive(tall[4] + late)
        yield


def iota(shape, axis):
    return lax.broadcasted_iota(jnp.int32, shape, axis)


def pick(mask, rows):
    ones = jnp.where(mask, 1.0, 0.0).astype(BF)
    return jnp.dot(ones, rows, preferred_element_type=F32).astype(BF)


def kernel(
    tokens, w, keep, count, out,
    wbuf, kv, feats, cbuf, slots, send1, recv1, send2, recv2, scores, heads, fin,
    send_sem, recv_sem, local_sem,
):
    s, z = lax.axis_index("seq"), lax.axis_index("tp")
    c = s % 2
    x = (s // 2) % NX
    y = s // (2 * NX)
    chip = s // 2
    e = s % 8

    def dev(yy, xx):
        return ((yy * NX + xx) * 2 + c, z)

    sibling = (s + 1 - 2 * c, z)
    y_peers = [(y + k) % NY for k in range(1, NY)]
    row_peers = [(e + k) % 8 for k in range(1, 8)]
    z_order = (1, 7, 2, 6, 3, 5, 4)
    z_peers = [(z + k) % NZ for k in z_order]

    barrier = pltpu.get_barrier_semaphore()
    greet = [(p * 8 + e, z) for p in y_peers]
    greet += [(y * 8 + p, z) for p in row_peers]
    greet += [(s, p) for p in z_peers]
    for device in greet:
        pl.semaphore_signal(barrier, inc=1, device_id=device, device_id_type=MESH)
    cbuf[y, e] = jnp.full((1, 128), count[0], jnp.int32)
    pl.semaphore_wait(barrier, len(greet))

    links = Links(send_sem, recv_sem)

    counts1 = [
        links.send(cbuf.at[y, e], cbuf.at[y, e], (y * 8 + p, z)) for p in row_peers
    ]

    mine, other = pl.multiple_of(c * HD, HD), pl.multiple_of((1 - c) * HD, HD)
    half = pl.ds(pl.multiple_of(c * 64, 64), 64)
    swap, local = [], []
    for g in range(3):
        place = wbuf.at[y, x, half, pl.ds(g * HD, HD)]
        swap.append(links.send(w.at[g, :, pl.ds(other, HD)], place, sibling))
        local.append(
            pltpu.make_async_copy(w.at[g, :, pl.ds(mine, HD)], place, local_sem.at[g])
        )
        local[-1].start()

    chosen = (iota((256, 128), 0) == keep[...]).astype(F32).astype(BF)
    slots[...] = lax.dot_general(
        chosen, tokens[...], (((0,), (0,)), ((), ())), preferred_element_type=F32
    ).astype(BF)

    for copy in local:
        copy.wait()
    for copy in swap:
        copy.wait_recv()
    gather = Gather(links, wbuf, (x, y, dev)).steps()
    next(gather)

    for copy in counts1:
        copy.wait_recv()
    counts2 = [links.send(cbuf.at[y], cbuf.at[y], (p * 8 + e, z)) for p in y_peers]
    next(gather)
    for copy in counts2:
        copy.wait_recv()

    counts = cbuf[...].reshape(64, 128)
    shard = iota((64, 128), 0)
    start = jnp.sum(jnp.where(shard < s, counts, 0), axis=0, keepdims=True)
    total = jnp.sum(jnp.where(shard == s, counts, 0), axis=0, keepdims=True)
    r, i = iota((128, 128), 0), iota((128, 128), 1)
    hit = (r // 2 == (start + i) % 64) & (r % 2 == i // 64) & (i < total)
    send1[...] = pick(hit, slots[...]).reshape(8, 16, 512)
    stage1 = [links.send(send1.at[p], recv1.at[y], (p * 8 + e, z)) for p in y_peers]
    own1 = pltpu.make_async_copy(send1.at[y], recv1.at[y], local_sem.at[3])
    own1.start()
    next(gather)
    next(gather)
    own1.wait()
    for copy in stage1:
        copy.wait_recv()
    turn = (r // 16 == (i // 2) % 8) & ((r // 2) % 8 == i // 16) & (r % 2 == i % 2)
    send2[...] = pick(turn, recv1[...].reshape(128, 512)).reshape(8, 16, 512)
    stage2 = [links.send(send2.at[p], recv2.at[e], (y * 8 + p, z)) for p in row_peers]
    own2 = pltpu.make_async_copy(send2.at[e], recv2.at[e], local_sem.at[4])
    own2.start()
    next(gather)
    next(gather)
    own2.wait()
    for copy in stage2:
        copy.wait_recv()
    lane = iota((64, 128), 1)
    source = ((lane // 2) % 8) * 8 + lane // 16
    begin = jnp.sum(jnp.where(shard < source, counts, 0), axis=0, keepdims=True)
    size = jnp.sum(jnp.where(shard == source, counts, 0), axis=0, keepdims=True)
    within = shard * 64 + s - begin
    live = (within >= 0) & (within < size) & ((within >= 64) == (lane % 2 == 1))
    feats[z, c] = pick(live, recv2[...].reshape(128, 512))

    over_z = [links.send(feats.at[z, c], feats.at[z, c], (s, p)) for p in z_peers]
    beside = [links.send(feats.at[z, c], feats.at[z, c], sibling)]
    for _ in range(3):
        next(gather)
    for k, copy in zip(z_order, over_z):
        copy.wait_recv()
        piece = feats.at[(z - k + NZ) % NZ, c]
        beside.append(links.send(piece, piece, sibling))
        if k in (7, 6, 5):
            next(gather)
    for _ in gather:
        pass
    for copy in beside:
        copy.wait_recv()

    def project(zz, acc):
        rows = feats[zz].reshape(128, 512)
        return acc + jnp.dot(rows, wbuf[zz].reshape(512, 384), preferred_element_type=F32)

    acc = lax.fori_loop(0, NZ, project, jnp.zeros((128, 384), F32))
    query = acc[:, :HD].astype(BF)
    kv[y, x] = acc[:, HD:].astype(BF)

    for _ in Gather(links, kv, (x, y, dev)).steps():
        pass

    qi, kj = iota((128, 512), 0), iota((128, 512), 1)
    rank_q = (qi % 64) * 64 + chip * 2 + qi // 64
    rank_k = (kj % 64) * 64 + (kj // 128) * 2 + (kj // 64) % 2
    scale = HD ** (-0.5)

    def score(yy, top):
        keys = kv[yy, :, :, :HD].reshape(512, HD)
        dots = lax.dot_general(
            query, keys, (((1,), (1,)), ((), ())), preferred_element_type=F32
        ) * scale
        dots = jnp.where(rank_k + yy * 8 > rank_q, -jnp.inf, dots)
        scores[yy] = dots
        return jnp.maximum(top, jnp.max(dots, axis=1, keepdims=True))

    top = lax.fori_loop(0, NY, score, jnp.full((128, 1), -jnp.inf, F32))

    def weigh(yy, carry):
        denom, numer = carry
        expo = jnp.exp(scores[yy] - top)
        values = kv[yy, :, :, HD:].reshape(512, HD)
        numer = numer + jnp.dot(expo.astype(BF), values, preferred_element_type=F32)
        return denom + jnp.sum(expo, axis=1, keepdims=True), numer

    denom, numer = lax.fori_loop(
        0, NY, weigh, (jnp.zeros((128, 1), F32), jnp.zeros((128, HD), F32))
    )
    heads[...] = (numer / denom).astype(BF).reshape(2, 64, HD)

    last = links.send(heads.at[1 - c], fin.at[c], sibling)
    own = pltpu.make_async_copy(heads.at[c], fin.at[c], local_sem.at[5])
    own.start()
    own.wait()
    last.wait_recv()
    out[:, :HD] = fin[0]
    out[:, HD:] = fin[1]
    links.drain()


def on_device(tokens, w_qkv, keep_list, counts):
    vmem = pl.BlockSpec(memory_space=pltpu.VMEM)
    return pl.pallas_call(
        kernel,
        out_shape=jax.ShapeDtypeStruct((64, 256), BF),
        in_specs=[
            vmem,
            pl.BlockSpec(memory_space=pl.ANY),
            vmem,
            pl.BlockSpec(memory_space=pltpu.SMEM),
        ],
        out_specs=vmem,
        scratch_shapes=[
            pltpu.VMEM((NY, NX, 128, 384), BF),
            pltpu.VMEM((NY, NX, 128, 256), BF),
            pltpu.VMEM((NZ, 2, 64, 512), BF),
            pltpu.VMEM((8, 8, 1, 128), jnp.int32),
            pltpu.VMEM((128, 512), BF),
            pltpu.VMEM((8, 16, 512), BF),
            pltpu.VMEM((8, 16, 512), BF),
            pltpu.VMEM((8, 16, 512), BF),
            pltpu.VMEM((8, 16, 512), BF),
            pltpu.VMEM((8, 128, 512), F32),
            pltpu.VMEM((2, 64, HD), BF),
            pltpu.VMEM((2, 64, HD), BF),
            pltpu.SemaphoreType.DMA((SEMS,)),
            pltpu.SemaphoreType.DMA((SEMS,)),
            pltpu.SemaphoreType.DMA((8,)),
        ],
        compiler_params=pltpu.CompilerParams(
            collective_id=0, has_side_effects=True, vmem_limit_bytes=48 * 1024 * 1024
        ),
    )(tokens, jnp.transpose(w_qkv, (1, 0, 2)), keep_list.reshape(1, 128), counts)


def solution(mesh):
    in_specs = (P("seq", "tp"), P("seq", None, "tp"), P("seq"), P("seq"))
    return jax.shard_map(
        on_device, mesh=mesh, in_specs=in_specs, out_specs=P("seq", "tp"), check_vma=False
    )
```

```python
import heapq

import jax
import jax.numpy as jnp
from jax import lax
from jax.experimental import pallas as pl
from jax.experimental.pallas import tpu as pltpu
from jax.sharding import PartitionSpec as P

MESH = pl.DeviceIdType.MESH
NX, NY, NZ = 4, 8, 8
HD = 128
BF = jnp.bfloat16
F32 = jnp.float32
I32 = jnp.int32
SEMS = 352
PEERS = sorted(
    ((dy, dx, dc) for dy in range(NY) for dx in range(NX) for dc in range(2) if dy or dx or dc),
    key=lambda p: -min(p[0], NY - p[0]) - min(p[1], NX - p[1]),
)


class Links:
    def __init__(self, send_sem, recv_sem):
        self.send_sem, self.recv_sem, self.count, self.copies = send_sem, recv_sem, 0, []

    def send(self, src, dst, device):
        copy = pltpu.make_async_remote_copy(
            src_ref=src,
            dst_ref=dst,
            send_sem=self.send_sem.at[self.count],
            recv_sem=self.recv_sem.at[self.count],
            device_id=device,
            device_id_type=MESH,
        )
        self.count += 1
        copy.start()
        self.copies.append(copy)
        return copy

    def drain(self):
        for copy in self.copies:
            copy.wait_send()


class Gather:
    ONE, ONE_A, ONE_B = (0, 48), (0, 32), (32, 48)
    TWO, TWO_A, TWO_B = (48, 128), (48, 96), (96, 128)

    def __init__(self, links, buf, place, unit):
        self.links, self.buf, self.unit = links, buf, unit
        self.x, self.y, self.dev = place
        self.clock, self.busy, self.queue, self.number = 0.0, {}, [], 0

    def col(self, k):
        return (self.x + k + NX) % NX

    def row(self, k):
        return (self.y + k + NY) % NY

    def send(self, row, col, rows, step):
        lo, hi = rows
        piece = self.buf.at[self.row(row), self.col(col), pl.ds(lo, hi - lo)]
        sy, sx = step
        copy = self.links.send(piece, piece, self.dev(self.row(sy), self.col(sx)))
        self.clock += 0.06
        hops = abs(sy) + abs(sx)
        way = (sy > 0, sy < 0, sx > 0, sx < 0)
        end = max(self.busy.get(way, 0.0), self.clock) + (hi - lo) / 128 * self.unit * hops
        self.busy[way] = end
        return copy, end + 1.95 + 0.65 * hops

    def when(self, sent, then):
        self.number += 1
        entry = (max(t for _, t in sent), self.number, [copy for copy, _ in sent], then)
        heapq.heappush(self.queue, entry)

    def advance(self, until):
        while self.queue and self.queue[0][0] <= until:
            at, _, copies, then = heapq.heappop(self.queue)
            for copy in copies:
                copy.wait_recv()
            self.clock = max(self.clock, at)
            then()

    def finish(self):
        self.advance(1e9)

    def ring_y(self, col, k=0):
        up = self.ONE_A if k == 3 else self.ONE
        down = self.ONE_B if k == 3 else self.ONE
        sent = [self.send(-k, col, up, (1, 0)), self.send(k, col, down, (-1, 0))]
        self.when(sent, (lambda: self.ring_y(col, k + 1)) if k < 3 else (lambda: None))

    def tree_y(self):
        far = [self.send(0, 0, self.TWO, (2, 0)), self.send(0, 0, self.TWO, (-2, 0))]
        near = [self.send(0, 0, self.TWO, (1, 0)), self.send(0, 0, self.TWO, (-1, 0))]

        def arrived():
            last = [self.send(-2, 0, self.TWO_A, (2, 0)), self.send(2, 0, self.TWO_B, (-2, 0))]
            third = [self.send(-2, 0, self.TWO, (1, 0)), self.send(2, 0, self.TWO, (-1, 0))]
            self.when(third, lambda: self.ring_x((-3, 3)))
            self.when(last, lambda: self.ring_x((4,)))
            self.ring_x((-2, 2))

        self.when(near, lambda: self.ring_x((-1, 1)))
        self.when(far, arrived)

    def ring_x(self, rows):
        sent = []
        for r in rows:
            sent += [self.send(r, 0, self.TWO, (0, 1)), self.send(r, 0, self.TWO, (0, -1))]

        def arrived():
            rest = []
            for r in rows:
                rest += [self.send(r, -1, self.TWO_A, (0, 1)), self.send(r, 1, self.TWO_B, (0, -1))]
            self.when(rest, lambda: None)

        self.when(sent, arrived)

    def start(self):
        sent = [self.send(0, 0, self.ONE, (0, 1)), self.send(0, 0, self.ONE, (0, -1))]

        def arrived():
            rest = [self.send(0, -1, self.ONE_A, (0, 1)), self.send(0, 1, self.ONE_B, (0, -1))]
            self.when(rest, lambda: self.ring_y(2))
            self.ring_y(-1)
            self.ring_y(1)

        self.when(sent, arrived)
        self.tree_y()
        self.ring_x((0,))
        self.ring_y(0)


def iota(shape, axis):
    return lax.broadcasted_iota(I32, shape, axis)


def pick(mask, rows):
    ones = jnp.where(mask, 1.0, 0.0).astype(BF)
    return jnp.dot(ones, rows, preferred_element_type=F32).astype(BF)


def kernel(
    tokens_hbm, w, keep_hbm, count_hbm, out,
    tokens, keep, count, wbuf, kv, feats, cbuf, slots, outbox, inbox, scores, heads, fin,
    send_sem, recv_sem, local_sem,
):
    s, z = lax.axis_index("seq"), lax.axis_index("tp")
    c = s % 2
    x = (s // 2) % NX
    y = s // (2 * NX)
    chip = s // 2

    def dev(yy, xx):
        return ((yy * NX + xx) * 2 + c, z)

    sibling = (s + 1 - 2 * c, z)
    peers = [(((y + p) % NY) * NX + (x + q) % NX) * 2 + (c + r) % 2 for p, q, r in PEERS]
    above = [(z + k) % NZ for k in range(NZ)]

    barrier = pltpu.get_barrier_semaphore()
    greet = [(p, z) for p in peers] + [(s, p) for p in above[1:]]
    for device in greet:
        pl.semaphore_signal(barrier, inc=1, device_id=device, device_id_type=MESH)

    mine, other = pl.multiple_of(c * HD, HD), pl.multiple_of((1 - c) * HD, HD)
    half = pl.ds(pl.multiple_of(c * 64, 64), 64)
    place = [wbuf.at[y, x, half, pl.ds(g * HD, HD)] for g in range(3)]
    local = [
        pltpu.make_async_copy(count_hbm, count, local_sem.at[0]),
        pltpu.make_async_copy(keep_hbm, keep, local_sem.at[1]),
        pltpu.make_async_copy(tokens_hbm, tokens, local_sem.at[2]),
    ]
    for g in range(3):
        local.append(
            pltpu.make_async_copy(w.at[g, :, pl.ds(mine, HD)], place[g], local_sem.at[3 + g])
        )
    for copy in local:
        copy.start()
    for copy in local:
        copy.wait()
    cbuf[s] = jnp.full((1, 128), count[0], I32)
    chosen = (iota((256, 128), 0) == keep[...]).astype(F32).astype(BF)
    rows = lax.dot_general(
        chosen, tokens[...], (((0,), (0,)), ((), ())), preferred_element_type=F32
    ).astype(BF)
    for q in range(4):
        slots[q * 128 : (q + 1) * 128] = rows[:, q * 128 : (q + 1) * 128]
    pl.semaphore_wait(barrier, len(greet))

    links = Links(send_sem, recv_sem)
    told = [links.send(cbuf.at[s], cbuf.at[s], (p, z)) for p in peers]
    swap = [links.send(w.at[g, :, pl.ds(other, HD)], place[g], sibling) for g in range(3)]
    for copy in swap:
        copy.wait_recv()
    gather = Gather(links, wbuf, (x, y, dev), 1.97)
    gather.start()
    gather.advance(3.5)
    for copy in told:
        copy.wait_recv()

    counts = cbuf[...].reshape(64, 128)
    shard = iota((64, 128), 0)
    begin = jnp.sum(jnp.where(shard < s, counts, 0), axis=0, keepdims=True)
    total = jnp.sum(jnp.where(shard == s, counts, 0), axis=0, keepdims=True)
    i = iota((1, 128), 1)
    code = jnp.where(i < total, ((begin + i) & 63) * 8 + (i >> 6), -8)
    code = jnp.concatenate([code + q * 2 for q in range(4)], axis=1)
    outbox[...] = pick(iota((512, 512), 0) == code, slots[...]).reshape(64, 8, 128)
    post = [links.send(outbox.at[p], inbox.at[s], (p, z)) for p in peers]
    own = pltpu.make_async_copy(outbox.at[s], inbox.at[s], local_sem.at[6])
    own.start()
    gather.advance(12.0)
    own.wait()
    wide = jnp.concatenate([counts] * 4, axis=1)
    shard, lane = iota((64, 512), 0), iota((64, 512), 1)
    begin = jnp.sum(jnp.where(shard < (lane >> 3), wide, 0), axis=0, keepdims=True)
    size = jnp.sum(jnp.where(shard == (lane >> 3), wide, 0), axis=0, keepdims=True)
    within = shard * 64 + s - begin
    live = (within >= 0) & (within < size) & ((within >> 6) == (lane & 1))
    block = (lane >> 1) & 3
    take = jnp.concatenate([live & (block == q) for q in range(4)], axis=0)
    for copy in post:
        copy.wait_recv()
    kept = pick(take, inbox[...].reshape(512, 128))
    feats[z, c] = jnp.concatenate([kept[q * 64 : (q + 1) * 64] for q in range(4)], axis=1)

    def over_z(k, lo, hi, step):
        piece = feats.at[above[k % NZ], c, pl.ds(lo, hi - lo)]
        return links.send(piece, piece, (s, above[step % NZ]))

    beside = {}

    def hand(k):
        piece = feats.at[above[k % NZ], c]
        beside[k] = links.send(piece, piece, sibling)

    pair2 = [over_z(0, 0, 64, 2), over_z(0, 0, 64, -2)]
    pair1 = [over_z(0, 0, 64, 1), over_z(0, 0, 64, -1)]
    hand(0)
    gather.advance(18.0)
    for copy in pair2:
        copy.wait_recv()
    pair4 = [over_z(-2, 0, 32, 2), over_z(2, 32, 64, -2)]
    pair3 = [over_z(-2, 0, 64, 1), over_z(2, 0, 64, -1)]
    hand(-2)
    hand(2)
    for copy in pair1:
        copy.wait_recv()
    hand(-1)
    hand(1)
    gather.finish()

    acc = jnp.zeros((128, 384), F32)

    def project(acc, k):
        beside[k].wait_recv()
        zz = above[k % NZ]
        block = feats[zz].reshape(128, 512)
        return acc + jnp.dot(block, wbuf[zz].reshape(512, 384), preferred_element_type=F32)

    for k in (0, -2, 2, -1, 1):
        acc = project(acc, k)
    for copy in pair3:
        copy.wait_recv()
    hand(-3)
    hand(3)
    for copy in pair4:
        copy.wait_recv()
    hand(4)
    for k in (-3, 3, 4):
        acc = project(acc, k)
    query = acc[:, :HD].astype(BF)
    kv[y, x] = acc[:, HD:].astype(BF)

    gather = Gather(links, kv, (x, y, dev), 1.31)
    gather.start()
    gather.finish()

    qi, kj = iota((128, 512), 0), iota((128, 512), 1)
    rank_q = (qi & 63) * 64 + chip * 2 + (qi >> 6)
    rank_k = (kj & 63) * 64 + (kj >> 7) * 2 + ((kj >> 6) & 1)
    scale = HD ** (-0.5)

    def score(yy, top):
        keys = kv[yy, :, :, :HD].reshape(512, HD)
        dots = lax.dot_general(
            query, keys, (((1,), (1,)), ((), ())), preferred_element_type=F32
        ) * scale
        dots = jnp.where(rank_k + yy * 8 > rank_q, -jnp.inf, dots)
        scores[yy] = dots
        return jnp.maximum(top, jnp.max(dots, axis=1, keepdims=True))

    top = lax.fori_loop(0, NY, score, jnp.full((128, 1), -jnp.inf, F32))

    def weigh(yy, carry):
        denom, numer = carry
        expo = jnp.exp(scores[yy] - top)
        values = kv[yy, :, :, HD:].reshape(512, HD)
        numer = numer + jnp.dot(expo.astype(BF), values, preferred_element_type=F32)
        return denom + jnp.sum(expo, axis=1, keepdims=True), numer

    denom, numer = lax.fori_loop(
        0, NY, weigh, (jnp.zeros((128, 1), F32), jnp.zeros((128, HD), F32))
    )
    heads[...] = (numer / denom).astype(BF).reshape(2, 64, HD)

    last = links.send(heads.at[1 - c], fin.at[c], sibling)
    own = pltpu.make_async_copy(heads.at[c], fin.at[c], local_sem.at[7])
    own.start()
    own.wait()
    last.wait_recv()
    out[:, :HD] = fin[0]
    out[:, HD:] = fin[1]
    links.drain()


def on_device(tokens, w_qkv, keep_list, counts):
    hbm = pl.BlockSpec(memory_space=pltpu.HBM)
    return pl.pallas_call(
        kernel,
        out_shape=jax.ShapeDtypeStruct((64, 256), BF),
        in_specs=[hbm] * 4,
        out_specs=pl.BlockSpec(memory_space=pltpu.VMEM),
        scratch_shapes=[
            pltpu.VMEM((256, 512), BF),
            pltpu.VMEM((1, 128), I32),
            pltpu.SMEM((1,), I32),
            pltpu.VMEM((NY, NX, 128, 384), BF),
            pltpu.VMEM((NY, NX, 128, 256), BF),
            pltpu.VMEM((NZ, 2, 64, 512), BF),
            pltpu.VMEM((64, 1, 128), I32),
            pltpu.VMEM((512, 128), BF),
            pltpu.VMEM((64, 8, 128), BF),
            pltpu.VMEM((64, 8, 128), BF),
            pltpu.VMEM((8, 128, 512), F32),
            pltpu.VMEM((2, 64, HD), BF),
            pltpu.VMEM((2, 64, HD), BF),
            pltpu.SemaphoreType.DMA((SEMS,)),
            pltpu.SemaphoreType.DMA((SEMS,)),
            pltpu.SemaphoreType.DMA((8,)),
        ],
        compiler_params=pltpu.CompilerParams(
            collective_id=0, has_side_effects=True, vmem_limit_bytes=60 * 1024 * 1024
        ),
    )(tokens, jnp.transpose(w_qkv, (1, 0, 2)), keep_list.reshape(1, 128), counts)


def solution(mesh):
    in_specs = (P("seq", "tp"), P("seq", None, "tp"), P("seq"), P("seq"))
    return jax.shard_map(
        on_device, mesh=mesh, in_specs=in_specs, out_specs=P("seq", "tp"), check_vma=False
    )
```

```python
import heapq

import jax
import jax.numpy as jnp
from jax import lax
from jax.experimental import pallas as pl
from jax.experimental.pallas import tpu as pltpu
from jax.sharding import PartitionSpec as P

MESH = pl.DeviceIdType.MESH
NX, NY, NZ = 4, 8, 8
HD = 128
BF = jnp.bfloat16
F32 = jnp.float32
I32 = jnp.int32
GROUPS = 96
PHASES = 8
PEERS = sorted(
    ((dy, dx, dc) for dy in range(NY) for dx in range(NX) for dc in range(2) if dy or dx or dc),
    key=lambda p: -min(p[0], NY - p[0]) - min(p[1], NX - p[1]),
)


class Links:
    def __init__(self, send_sem, recv_sem):
        self.send_sem, self.recv_sem, self.phases, self.count = send_sem, recv_sem, 0, 0

    def group(self):
        self.count += 1
        return self.recv_sem.at[self.count - 1]

    def phase(self):
        self.phases += 1
        return self.send_sem.at[self.phases - 1]

    def send(self, src, dst, device, group, phase):
        pltpu.make_async_remote_copy(
            src_ref=src,
            dst_ref=dst,
            send_sem=phase,
            recv_sem=group,
            device_id=device,
            device_id_type=MESH,
        ).start()


def await_bytes(size, semaphore):
    pltpu.make_async_copy(size, size, semaphore).wait()


class Gather:
    ONE, ONE_A, ONE_B = (0, 48), (0, 32), (32, 48)
    TWO, TWO_A, TWO_B = (48, 128), (48, 96), (96, 128)

    def __init__(self, links, buf, place, unit, complete=None):
        self.links, self.buf, self.unit, self.complete = links, buf, unit, complete
        self.phase = links.phase()
        self.x, self.y, self.dev = place
        self.clock, self.busy, self.queue, self.number = 0.0, {}, [], 0
        self.missing = {0: 3, 1: 5, 2: 5, 3: 5, 4: 5}

    def col(self, k):
        return (self.x + k + NX) % NX

    def row(self, k):
        return (self.y + k + NY) % NY

    def send(self, group, row, col, rows, step):
        lo, hi = rows
        piece = self.buf.at[self.row(row) * NX + self.col(col), pl.ds(lo, hi - lo)]
        sy, sx = step
        to = self.dev(self.row(sy), self.col(sx))
        self.links.send(piece, piece, to, group[0], self.phase)
        self.clock += 0.06
        hops = abs(sy) + abs(sx)
        way = (sy > 0, sy < 0, sx > 0, sx < 0)
        end = max(self.busy.get(way, 0.0), self.clock) + (hi - lo) / 128 * self.unit * hops
        self.busy[way] = end
        group[1] = max(group[1], end + 1.95 + 0.65 * hops)
        group[2] += hi - lo

    def group(self):
        return [self.links.group(), 0.0, 0]

    def when(self, group, then):
        self.number += 1
        heapq.heappush(self.queue, (group[1], self.number, group, then))

    def advance(self, until):
        while self.queue and self.queue[0][0] <= until:
            at, _, (semaphore, _, rows), then = heapq.heappop(self.queue)
            blocks = 1 if rows <= 128 else rows // 80
            await_bytes(self.buf.at[pl.ds(0, blocks), pl.ds(0, rows // blocks)], semaphore)
            self.clock = max(self.clock, at)
            then()

    def finish(self):
        self.advance(1e9)

    def done(self, k):
        self.missing[k] -= 1
        if not self.missing[k] and self.complete:
            self.complete(k)

    def ring_y(self, cols, k=0):
        up = self.ONE_A if k == 3 else self.ONE
        down = self.ONE_B if k == 3 else self.ONE
        for col in cols:
            group = self.group()
            self.send(group, -k, col, up, (1, 0))
            self.send(group, k, col, down, (-1, 0))

            def arrived(col=col):
                if k < 3:
                    self.ring_y((col,), k + 1)
                self.done(k + 1)

            self.when(group, arrived)

    def tree_y(self):
        far, near = self.group(), self.group()
        self.send(far, 0, 0, self.TWO, (2, 0))
        self.send(far, 0, 0, self.TWO, (-2, 0))
        self.send(near, 0, 0, self.TWO, (1, 0))
        self.send(near, 0, 0, self.TWO, (-1, 0))

        def arrived():
            last, third = self.group(), self.group()
            self.send(last, -2, 0, self.TWO_A, (2, 0))
            self.send(last, 2, 0, self.TWO_B, (-2, 0))
            self.send(third, -2, 0, self.TWO, (1, 0))
            self.send(third, 2, 0, self.TWO, (-1, 0))
            self.when(third, lambda: self.ring_x((-3, 3)))
            self.when(last, lambda: self.ring_x((4,)))
            self.ring_x((-2, 2))

        self.when(near, lambda: self.ring_x((-1, 1)))
        self.when(far, arrived)

    def ring_x(self, rows):
        group = self.group()
        for r in rows:
            self.send(group, r, 0, self.TWO, (0, 1))
            self.send(group, r, 0, self.TWO, (0, -1))

        def arrived():
            rest = self.group()
            for r in rows:
                self.send(rest, r, -1, self.TWO_A, (0, 1))
                self.send(rest, r, 1, self.TWO_B, (0, -1))
            self.when(rest, lambda: self.done(abs(rows[0])))

        self.when(group, arrived)

    def start(self):
        group = self.group()
        self.send(group, 0, 0, self.ONE, (0, 1))
        self.send(group, 0, 0, self.ONE, (0, -1))

        def arrived():
            rest = self.group()
            self.send(rest, 0, -1, self.ONE_A, (0, 1))
            self.send(rest, 0, 1, self.ONE_B, (0, -1))

            def across():
                self.ring_y((2,))
                self.done(0)

            self.when(rest, across)
            self.ring_y((-1, 1))
            self.done(0)

        self.when(group, arrived)
        self.tree_y()
        self.ring_x((0,))
        self.ring_y((0,))


def iota(shape, axis):
    return lax.broadcasted_iota(I32, shape, axis)


def pick(mask, rows):
    ones = jnp.where(mask, 1.0, 0.0).astype(BF)
    return jnp.dot(ones, rows, preferred_element_type=F32).astype(BF)


def kernel(
    tokens_hbm, w, keep_hbm, count_hbm, out,
    tokens, keep, count, wbuf, kv, feats, cbuf, slots, outbox, inbox, heads, fin,
    send_sem, recv_sem, local_sem,
):
    s, z = lax.axis_index("seq"), lax.axis_index("tp")
    c = s % 2
    x = (s // 2) % NX
    y = s // (2 * NX)
    chip = s // 2

    def dev(yy, xx):
        return ((yy * NX + xx) * 2 + c, z)

    sibling = (s + 1 - 2 * c, z)
    peers = [(((y + p) % NY) * NX + (x + q) % NX) * 2 + (c + r) % 2 for p, q, r in PEERS]
    above = [(z + k) % NZ for k in range(NZ)]

    barrier = pltpu.get_barrier_semaphore()
    greet = [(p, z) for p in peers] + [(s, p) for p in above[1:]]
    for device in greet:
        pl.semaphore_signal(barrier, inc=1, device_id=device, device_id_type=MESH)

    mine, other = pl.multiple_of(c * HD, HD), pl.multiple_of((1 - c) * HD, HD)
    half = pl.ds(pl.multiple_of(c * 64, 64), 64)
    place = [wbuf.at[chip, half, pl.ds(g * HD, HD)] for g in range(3)]
    local = [
        pltpu.make_async_copy(count_hbm, count, local_sem.at[0]),
        pltpu.make_async_copy(keep_hbm, keep, local_sem.at[1]),
        pltpu.make_async_copy(tokens_hbm, tokens, local_sem.at[2]),
    ]
    for g in range(3):
        local.append(
            pltpu.make_async_copy(w.at[g, :, pl.ds(mine, HD)], place[g], local_sem.at[3 + g])
        )
    for copy in local:
        copy.start()
    for copy in local:
        copy.wait()
    cbuf[s] = jnp.full((1, 128), count[0], I32)
    chosen = (iota((256, 128), 0) == keep[...]).astype(F32).astype(BF)
    rows = lax.dot_general(
        chosen, tokens[...], (((0,), (0,)), ((), ())), preferred_element_type=F32
    ).astype(BF)
    for q in range(4):
        slots[q * 128 : (q + 1) * 128] = rows[:, q * 128 : (q + 1) * 128]
    pl.semaphore_wait(barrier, len(greet))

    links = Links(send_sem, recv_sem)
    rest = pl.ds(0, len(peers))
    swap_out, told_out, post_out, z_out, last_out = [links.phase() for _ in range(5)]

    swapped = links.group()
    for g in range(3):
        links.send(w.at[g, :, pl.ds(other, HD)], place[g], sibling, swapped, swap_out)
    told = links.group()
    for p in peers:
        links.send(cbuf.at[s], cbuf.at[s], (p, z), told, told_out)
    await_bytes(wbuf.at[0, pl.ds(0, 64)], swapped)
    weights = gather = Gather(links, wbuf, (x, y, dev), 1.97)
    gather.start()
    gather.advance(2.8)
    await_bytes(cbuf.at[rest], told)

    counts = cbuf[...].reshape(64, 128)
    shard = iota((64, 128), 0)
    begin = jnp.sum(jnp.where(shard < s, counts, 0), axis=0, keepdims=True)
    total = jnp.sum(jnp.where(shard == s, counts, 0), axis=0, keepdims=True)
    i = iota((1, 128), 1)
    code = jnp.where(i < total, ((begin + i) & 63) * 8 + (i >> 6), -8)
    code = jnp.concatenate([code + q * 2 for q in range(4)], axis=1)
    outbox[...] = pick(iota((512, 512), 0) == code, slots[...]).reshape(64, 8, 128)
    post = links.group()
    own = pltpu.make_async_copy(outbox.at[s], inbox.at[s], local_sem.at[6])
    own.start()
    for part in range(4):
        for p in peers[part * 16 : part * 16 + 16]:
            links.send(outbox.at[p], inbox.at[s], (p, z), post, post_out)
        gather.advance(4.8 + part)
    gather.advance(10.0)
    own.wait()
    wide = jnp.concatenate([counts] * 4, axis=1)
    shard, lane = iota((64, 512), 0), iota((64, 512), 1)
    begin = jnp.sum(jnp.where(shard < (lane >> 3), wide, 0), axis=0, keepdims=True)
    size = jnp.sum(jnp.where(shard == (lane >> 3), wide, 0), axis=0, keepdims=True)
    within = shard * 64 + s - begin
    live = (within >= 0) & (within < size) & ((within >> 6) == (lane & 1))
    block = (lane >> 1) & 3
    take = jnp.concatenate([live & (block == q) for q in range(4)], axis=0)
    await_bytes(inbox.at[rest], post)
    kept = pick(take, inbox[...].reshape(512, 128))
    feats[z * 2 + c] = jnp.concatenate([kept[q * 64 : (q + 1) * 64] for q in range(4)], axis=1)

    def over_z(group, k, lo, hi, step):
        piece = feats.at[above[k % NZ] * 2 + c, pl.ds(lo, hi - lo)]
        links.send(piece, piece, (s, above[step % NZ]), group, z_out)

    beside = {}

    def hand(*ks):
        group = links.group()
        for k in ks:
            piece = feats.at[above[k % NZ] * 2 + c]
            links.send(piece, piece, sibling, group, z_out)
        beside[ks] = group

    pair2, pair1, pair3, pair4 = [links.group() for _ in range(4)]
    two = feats.at[pl.ds(0, 2)]
    for k in (2, -2):
        over_z(pair2, 0, 0, 64, k)
    for k in (1, -1):
        over_z(pair1, 0, 0, 64, k)
    hand(0)
    gather.advance(17.0)
    await_bytes(two, pair2)
    over_z(pair4, -2, 0, 32, 2)
    over_z(pair4, 2, 32, 64, -2)
    over_z(pair3, -2, 0, 64, 1)
    over_z(pair3, 2, 0, 64, -1)
    hand(-2, 2)
    await_bytes(two, pair1)
    hand(-1, 1)
    gather.finish()

    acc = jnp.zeros((128, 384), F32)

    def project(acc, *ks):
        await_bytes(feats.at[pl.ds(0, len(ks))], beside[ks])
        for k in ks:
            zz = above[k % NZ]
            block = feats[pl.ds(zz * 2, 2)].reshape(128, 512)
            weight = wbuf[pl.ds(zz * NX, NX)].reshape(512, 384)
            acc = acc + jnp.dot(block, weight, preferred_element_type=F32)
        return acc

    acc = project(acc, 0)
    acc = project(acc, -2, 2)
    acc = project(acc, -1, 1)
    await_bytes(two, pair3)
    hand(-3, 3)
    await_bytes(feats.at[0], pair4)
    hand(4)
    acc = project(acc, -3, 3)
    acc = project(acc, 4)
    query = acc[:, :HD].astype(BF)
    kv[chip] = acc[:, HD:].astype(BF)

    qi, kj = iota((128, 512), 0), iota((128, 512), 1)
    lead = (kj & 63) * 64 + (kj >> 7) * 2 + ((kj >> 6) & 1)
    lead = lead - (qi & 63) * 64 - (qi >> 6) - chip * 2
    scale = HD ** (-0.5) * 1.4426950408889634
    state = [
        jnp.full((128, 1), -1e30, F32),
        jnp.zeros((128, 1), F32),
        jnp.zeros((128, HD), F32),
    ]

    def attend(k):
        for kk in sorted({-k, k}):
            if kk == -4:
                continue
            yy = (y + kk + NY) % NY
            top, denom, numer = state
            block = kv[pl.ds(yy * NX, NX)].reshape(512, 2 * HD)
            dots = lax.dot_general(
                query, block[:, :HD], (((1,), (1,)), ((), ())), preferred_element_type=F32
            ) * scale
            dots = jnp.where(lead > yy * -8, -jnp.inf, dots)
            high = jnp.maximum(top, jnp.max(dots, axis=1, keepdims=True))
            fade = jnp.exp2(top - high)
            expo = jnp.exp2(dots - high)
            state[0] = high
            state[1] = denom * fade + jnp.sum(expo, axis=1, keepdims=True)
            state[2] = numer * fade + jnp.dot(
                expo.astype(BF), block[:, HD:], preferred_element_type=F32
            )

    gather = Gather(links, kv, (x, y, dev), 1.31, attend)
    gather.start()
    gather.finish()
    heads[...] = (state[2] / state[1]).astype(BF).reshape(2, 64, HD)

    last = links.group()
    links.send(heads.at[1 - c], fin.at[c], sibling, last, last_out)
    own = pltpu.make_async_copy(heads.at[c], fin.at[c], local_sem.at[7])
    own.start()
    own.wait()
    await_bytes(fin.at[0], last)
    out[:, :HD] = fin[0]
    out[:, HD:] = fin[1]
    blocks = pl.ds(0, NX * NY - 1)
    sent = [
        (wbuf.at[0, pl.ds(0, 64)], swap_out),
        (cbuf.at[rest], told_out),
        (inbox.at[rest], post_out),
        (wbuf.at[blocks], weights.phase),
        (feats.at[pl.ds(0, 2 * NZ - 1)], z_out),
        (kv.at[blocks], gather.phase),
        (heads.at[0], last_out),
    ]
    for size, semaphore in sent:
        await_bytes(size, semaphore)


def on_device(tokens, w_qkv, keep_list, counts):
    hbm = pl.BlockSpec(memory_space=pltpu.HBM)
    return pl.pallas_call(
        kernel,
        out_shape=jax.ShapeDtypeStruct((64, 256), BF),
        in_specs=[hbm] * 4,
        out_specs=pl.BlockSpec(memory_space=pltpu.VMEM),
        scratch_shapes=[
            pltpu.VMEM((256, 512), BF),
            pltpu.VMEM((1, 128), I32),
            pltpu.SMEM((1,), I32),
            pltpu.VMEM((NY * NX, 128, 384), BF),
            pltpu.VMEM((NY * NX, 128, 256), BF),
            pltpu.VMEM((NZ * 2, 64, 512), BF),
            pltpu.VMEM((64, 1, 128), I32),
            pltpu.VMEM((512, 128), BF),
            pltpu.VMEM((64, 8, 128), BF),
            pltpu.VMEM((64, 8, 128), BF),
            pltpu.VMEM((2, 64, HD), BF),
            pltpu.VMEM((2, 64, HD), BF),
            pltpu.SemaphoreType.DMA((PHASES,)),
            pltpu.SemaphoreType.DMA((GROUPS,)),
            pltpu.SemaphoreType.DMA((8,)),
        ],
        compiler_params=pltpu.CompilerParams(
            collective_id=0, has_side_effects=True, vmem_limit_bytes=60 * 1024 * 1024
        ),
    )(tokens, jnp.transpose(w_qkv, (1, 0, 2)), keep_list.reshape(1, 128), counts)


def solution(mesh):
    in_specs = (P("seq", "tp"), P("seq", None, "tp"), P("seq"), P("seq"))
    return jax.shard_map(
        on_device, mesh=mesh, in_specs=in_specs, out_specs=P("seq", "tp"), check_vma=False
    )
```

```python
import heapq

import jax
import jax.numpy as jnp
from jax import lax
from jax.experimental import pallas as pl
from jax.experimental.pallas import tpu as pltpu
from jax.sharding import PartitionSpec as P

MESH = pl.DeviceIdType.MESH
NX, NY, NZ = 4, 8, 8
HD = 128
BF = jnp.bfloat16
F32 = jnp.float32
I32 = jnp.int32
T1, T2, T3 = 2.8, 9.0, 17.0
GROUPS = 96
PHASES = 8
PEERS = sorted(
    ((dy, dx, dc) for dy in range(NY) for dx in range(NX) for dc in range(2) if dy or dx or dc),
    key=lambda p: -min(p[0], NY - p[0]) - min(p[1], NX - p[1]),
)


class Links:
    def __init__(self, send_sem, recv_sem):
        self.send_sem, self.recv_sem, self.phases, self.count = send_sem, recv_sem, 0, 0

    def group(self):
        self.count += 1
        return self.recv_sem.at[self.count - 1]

    def phase(self):
        self.phases += 1
        return self.send_sem.at[self.phases - 1]

    def send(self, src, dst, device, group, phase):
        pltpu.make_async_remote_copy(
            src_ref=src,
            dst_ref=dst,
            send_sem=phase,
            recv_sem=group,
            device_id=device,
            device_id_type=MESH,
        ).start()


def await_bytes(size, semaphore):
    pltpu.make_async_copy(size, size, semaphore).wait()


class Gather:
    ONE, ONE_A, ONE_B = (0, 48), (0, 32), (32, 48)
    TWO, TWO_A, TWO_B = (48, 128), (48, 96), (96, 128)

    def __init__(self, links, buf, place, unit, complete=None):
        self.links, self.buf, self.unit, self.complete = links, buf, unit, complete
        self.phase = links.phase()
        self.x, self.y, self.dev = place
        self.clock, self.busy, self.queue, self.number = 0.0, {}, [], 0
        self.missing = {0: 3, 1: 5, 2: 5, 3: 5, 4: 5}

    def col(self, k):
        return (self.x + k + NX) % NX

    def row(self, k):
        return (self.y + k + NY) % NY

    def send(self, group, row, col, rows, step):
        lo, hi = rows
        piece = self.buf.at[self.row(row) * NX + self.col(col), pl.ds(lo, hi - lo)]
        sy, sx = step
        to = self.dev(self.row(sy), self.col(sx))
        self.links.send(piece, piece, to, group[0], self.phase)
        self.clock += 0.06
        hops = abs(sy) + abs(sx)
        way = (sy > 0, sy < 0, sx > 0, sx < 0)
        end = max(self.busy.get(way, 0.0), self.clock) + (hi - lo) / 128 * self.unit * hops
        self.busy[way] = end
        group[1] = max(group[1], end + 1.95 + 0.65 * hops)
        group[2] += hi - lo

    def group(self):
        return [self.links.group(), 0.0, 0]

    def when(self, group, then):
        self.number += 1
        heapq.heappush(self.queue, (group[1], self.number, group, then))

    def advance(self, until):
        while self.queue and self.queue[0][0] <= until:
            at, _, (semaphore, _, rows), then = heapq.heappop(self.queue)
            blocks = 1 if rows <= 128 else rows // 80
            await_bytes(self.buf.at[pl.ds(0, blocks), pl.ds(0, rows // blocks)], semaphore)
            self.clock = max(self.clock, at)
            then()

    def finish(self):
        self.advance(1e9)

    def done(self, k):
        self.missing[k] -= 1
        if not self.missing[k] and self.complete:
            self.complete(k)

    def ring_y(self, cols, k=0):
        for col in cols:
            group = self.group()
            self.send(group, -k, col, self.ONE, (1, 0))
            self.send(group, k, col, self.ONE, (-1, 0))
            if k == 2:
                last = self.group()
                self.send(last, -2, col, self.ONE_A, (2, 0))
                self.send(last, 2, col, self.ONE_B, (-2, 0))
                self.when(last, lambda: self.done(4))

            def arrived(col=col):
                if k < 2:
                    self.ring_y((col,), k + 1)
                self.done(k + 1)

            self.when(group, arrived)

    def tree_y(self):
        far, near = self.group(), self.group()
        self.send(far, 0, 0, self.TWO, (2, 0))
        self.send(far, 0, 0, self.TWO, (-2, 0))
        self.send(near, 0, 0, self.TWO, (1, 0))
        self.send(near, 0, 0, self.TWO, (-1, 0))

        def arrived():
            last, third = self.group(), self.group()
            self.send(last, -2, 0, self.TWO_A, (2, 0))
            self.send(last, 2, 0, self.TWO_B, (-2, 0))
            self.send(third, -2, 0, self.TWO, (1, 0))
            self.send(third, 2, 0, self.TWO, (-1, 0))
            self.when(third, lambda: self.ring_x((-3, 3)))
            self.when(last, lambda: self.ring_x((4,)))
            self.ring_x((-2, 2))

        self.when(near, lambda: self.ring_x((-1, 1)))
        self.when(far, arrived)

    def ring_x(self, rows):
        group = self.group()
        for r in rows:
            self.send(group, r, 0, self.TWO, (0, 1))
            self.send(group, r, 0, self.TWO, (0, -1))

        def arrived():
            rest = self.group()
            for r in rows:
                self.send(rest, r, -1, self.TWO_A, (0, 1))
                self.send(rest, r, 1, self.TWO_B, (0, -1))
            self.when(rest, lambda: self.done(abs(rows[0])))

        self.when(group, arrived)

    def start(self):
        group = self.group()
        self.send(group, 0, 0, self.ONE, (0, 1))
        self.send(group, 0, 0, self.ONE, (0, -1))

        def arrived():
            rest = self.group()
            self.send(rest, 0, -1, self.ONE_A, (0, 1))
            self.send(rest, 0, 1, self.ONE_B, (0, -1))

            def across():
                self.ring_y((2,))
                self.done(0)

            self.when(rest, across)
            self.ring_y((-1, 1))
            self.done(0)

        self.when(group, arrived)
        self.tree_y()
        self.ring_x((0,))
        self.ring_y((0,))


def iota(shape, axis):
    return lax.broadcasted_iota(I32, shape, axis)


def pick(mask, rows):
    ones = jnp.where(mask, 1.0, 0.0).astype(BF)
    return jnp.dot(ones, rows, preferred_element_type=F32).astype(BF)


def kernel(
    tokens_hbm, w, keep_hbm, count_hbm, out,
    tokens, keep, count, wbuf, kv, feats, cbuf, slots, outbox, inbox, heads, fin,
    send_sem, recv_sem, local_sem,
):
    s, z = lax.axis_index("seq"), lax.axis_index("tp")
    c = s % 2
    x = (s // 2) % NX
    y = s // (2 * NX)
    chip = s // 2

    def dev(yy, xx):
        return ((yy * NX + xx) * 2 + c, z)

    sibling = (s + 1 - 2 * c, z)
    peers = [(((y + p) % NY) * NX + (x + q) % NX) * 2 + (c + r) % 2 for p, q, r in PEERS]
    above = [(z + k) % NZ for k in range(NZ)]

    barrier = pltpu.get_barrier_semaphore()
    greet = [(p, z) for p in peers] + [(s, p) for p in above[1:]]
    for device in greet:
        pl.semaphore_signal(barrier, inc=1, device_id=device, device_id_type=MESH)

    mine, other = pl.multiple_of(c * HD, HD), pl.multiple_of((1 - c) * HD, HD)
    half = pl.ds(pl.multiple_of(c * 64, 64), 64)
    place = [wbuf.at[chip, half, pl.ds(g * HD, HD)] for g in range(3)]
    local = [
        pltpu.make_async_copy(count_hbm, count, local_sem.at[0]),
        pltpu.make_async_copy(keep_hbm, keep, local_sem.at[1]),
        pltpu.make_async_copy(tokens_hbm, tokens, local_sem.at[2]),
    ]
    for g in range(3):
        local.append(
            pltpu.make_async_copy(w.at[g, :, pl.ds(mine, HD)], place[g], local_sem.at[3 + g])
        )
    for copy in local:
        copy.start()
    local[0].wait()
    cbuf[s] = jnp.full((1, 128), count[0], I32)
    pl.semaphore_wait(barrier, len(greet))

    links = Links(send_sem, recv_sem)
    rest = pl.ds(0, len(peers))
    swap_out, told_out, post_out, z_out, last_out = [links.phase() for _ in range(5)]

    swapped = links.group()
    for g in range(3):
        links.send(w.at[g, :, pl.ds(other, HD)], place[g], sibling, swapped, swap_out)
    told = links.group()
    for p in peers:
        links.send(cbuf.at[s], cbuf.at[s], (p, z), told, told_out)
    for copy in local[3:]:
        copy.wait()
    await_bytes(wbuf.at[0, pl.ds(0, 64)], swapped)
    weights = gather = Gather(links, wbuf, (x, y, dev), 1.97)
    gather.start()
    for copy in local[1:3]:
        copy.wait()
    chosen = (iota((256, 128), 0) == keep[...]).astype(F32).astype(BF)
    rows = lax.dot_general(
        chosen, tokens[...], (((0,), (0,)), ((), ())), preferred_element_type=F32
    ).astype(BF)
    for q in range(4):
        slots[q * 128 : (q + 1) * 128] = rows[:, q * 128 : (q + 1) * 128]
    gather.advance(T1)
    await_bytes(cbuf.at[rest], told)

    counts = cbuf[...].reshape(64, 128)
    shard = iota((64, 128), 0)
    begin = jnp.sum(jnp.where(shard < s, counts, 0), axis=0, keepdims=True)
    total = jnp.sum(jnp.where(shard == s, counts, 0), axis=0, keepdims=True)
    i = iota((1, 128), 1)
    code = jnp.where(i < total, ((begin + i) & 63) * 8 + (i >> 6), -8)
    code = jnp.concatenate([code + q * 2 for q in range(4)], axis=1)
    outbox[...] = pick(iota((512, 512), 0) == code, slots[...]).reshape(64, 8, 128)
    post = links.group()
    own = pltpu.make_async_copy(outbox.at[s], inbox.at[s], local_sem.at[6])
    own.start()
    for p in peers:
        links.send(outbox.at[p], inbox.at[s], (p, z), post, post_out)
    gather.advance(T2)
    own.wait()
    wide = jnp.concatenate([counts] * 4, axis=1)
    shard, lane = iota((64, 512), 0), iota((64, 512), 1)
    begin = jnp.sum(jnp.where(shard < (lane >> 3), wide, 0), axis=0, keepdims=True)
    size = jnp.sum(jnp.where(shard == (lane >> 3), wide, 0), axis=0, keepdims=True)
    within = shard * 64 + s - begin
    live = (within >= 0) & (within < size) & ((within >> 6) == (lane & 1))
    block = (lane >> 1) & 3
    take = jnp.concatenate([live & (block == q) for q in range(4)], axis=0)
    await_bytes(inbox.at[rest], post)
    kept = pick(take, inbox[...].reshape(512, 128))
    feats[z * 2 + c] = jnp.concatenate([kept[q * 64 : (q + 1) * 64] for q in range(4)], axis=1)

    def over_z(group, k, lo, hi, step):
        piece = feats.at[above[k % NZ] * 2 + c, pl.ds(lo, hi - lo)]
        links.send(piece, piece, (s, above[step % NZ]), group, z_out)

    beside = {}

    def hand(*ks):
        group = links.group()
        for k in ks:
            piece = feats.at[above[k % NZ] * 2 + c]
            links.send(piece, piece, sibling, group, z_out)
        beside[ks] = group

    pair2, pair1, pair3, pair4 = [links.group() for _ in range(4)]
    two = feats.at[pl.ds(0, 2)]
    for k in (2, -2):
        over_z(pair2, 0, 0, 64, k)
    for k in (1, -1):
        over_z(pair1, 0, 0, 64, k)
    hand(0)
    gather.advance(T3)
    await_bytes(two, pair2)
    over_z(pair4, -2, 0, 32, 2)
    over_z(pair4, 2, 32, 64, -2)
    over_z(pair3, -2, 0, 64, 1)
    over_z(pair3, 2, 0, 64, -1)
    hand(-2, 2)
    await_bytes(two, pair1)
    hand(-1, 1)
    gather.finish()

    acc = jnp.zeros((128, 384), F32)

    def project(acc, *ks):
        await_bytes(feats.at[pl.ds(0, len(ks))], beside[ks])
        for k in ks:
            zz = above[k % NZ]
            block = feats[pl.ds(zz * 2, 2)].reshape(128, 512)
            weight = wbuf[pl.ds(zz * NX, NX)].reshape(512, 384)
            acc = acc + jnp.dot(block, weight, preferred_element_type=F32)
        return acc

    acc = project(acc, 0)
    acc = project(acc, -2, 2)
    acc = project(acc, -1, 1)
    await_bytes(two, pair3)
    hand(-3, 3)
    await_bytes(feats.at[0], pair4)
    hand(4)
    acc = project(acc, -3, 3)
    acc = project(acc, 4)
    query = acc[:, :HD].astype(BF)
    kv[chip] = acc[:, HD:].astype(BF)

    qi, kj = iota((128, 512), 0), iota((128, 512), 1)
    lead = (kj & 63) * 64 + (kj >> 7) * 2 + ((kj >> 6) & 1)
    lead = lead - (qi & 63) * 64 - (qi >> 6) - chip * 2
    scale = HD ** (-0.5) * 1.4426950408889634
    state = [
        jnp.full((128, 1), -1e30, F32),
        jnp.zeros((128, 1), F32),
        jnp.zeros((128, HD), F32),
    ]

    def attend(k):
        for kk in sorted({-k, k}):
            if kk == -4:
                continue
            yy = (y + kk + NY) % NY
            top, denom, numer = state
            block = kv[pl.ds(yy * NX, NX)].reshape(512, 2 * HD)
            dots = lax.dot_general(
                query, block[:, :HD], (((1,), (1,)), ((), ())), preferred_element_type=F32
            ) * scale
            dots = jnp.where(lead > yy * -8, -jnp.inf, dots)
            high = jnp.maximum(top, jnp.max(dots, axis=1, keepdims=True))
            fade = jnp.exp2(top - high)
            expo = jnp.exp2(dots - high)
            state[0] = high
            state[1] = denom * fade + jnp.sum(expo, axis=1, keepdims=True)
            state[2] = numer * fade + jnp.dot(
                expo.astype(BF), block[:, HD:], preferred_element_type=F32
            )

    gather = Gather(links, kv, (x, y, dev), 1.31, attend)
    gather.start()
    gather.finish()
    heads[...] = (state[2] / state[1]).astype(BF).reshape(2, 64, HD)

    last = links.group()
    links.send(heads.at[1 - c], fin.at[c], sibling, last, last_out)
    own = pltpu.make_async_copy(heads.at[c], fin.at[c], local_sem.at[7])
    own.start()
    own.wait()
    await_bytes(fin.at[0], last)
    out[:, :HD] = fin[0]
    out[:, HD:] = fin[1]
    blocks = pl.ds(0, NX * NY - 1)
    sent = [
        (wbuf.at[0, pl.ds(0, 64)], swap_out),
        (cbuf.at[rest], told_out),
        (inbox.at[rest], post_out),
        (wbuf.at[blocks], weights.phase),
        (feats.at[pl.ds(0, 2 * NZ - 1)], z_out),
        (kv.at[blocks], gather.phase),
        (heads.at[0], last_out),
    ]
    for size, semaphore in sent:
        await_bytes(size, semaphore)


def on_device(tokens, w_qkv, keep_list, counts):
    hbm = pl.BlockSpec(memory_space=pltpu.HBM)
    return pl.pallas_call(
        kernel,
        out_shape=jax.ShapeDtypeStruct((64, 256), BF),
        in_specs=[hbm] * 4,
        out_specs=pl.BlockSpec(memory_space=pltpu.VMEM),
        scratch_shapes=[
            pltpu.VMEM((256, 512), BF),
            pltpu.VMEM((1, 128), I32),
            pltpu.SMEM((1,), I32),
            pltpu.VMEM((NY * NX, 128, 384), BF),
            pltpu.VMEM((NY * NX, 128, 256), BF),
            pltpu.VMEM((NZ * 2, 64, 512), BF),
            pltpu.VMEM((64, 1, 128), I32),
            pltpu.VMEM((512, 128), BF),
            pltpu.VMEM((64, 8, 128), BF),
            pltpu.VMEM((64, 8, 128), BF),
            pltpu.VMEM((2, 64, HD), BF),
            pltpu.VMEM((2, 64, HD), BF),
            pltpu.SemaphoreType.DMA((PHASES,)),
            pltpu.SemaphoreType.DMA((GROUPS,)),
            pltpu.SemaphoreType.DMA((8,)),
        ],
        compiler_params=pltpu.CompilerParams(
            collective_id=0, has_side_effects=True, vmem_limit_bytes=60 * 1024 * 1024
        ),
    )(tokens, jnp.transpose(w_qkv, (1, 0, 2)), keep_list.reshape(1, 128), counts)


def solution(mesh):
    in_specs = (P("seq", "tp"), P("seq", None, "tp"), P("seq"), P("seq"))
    return jax.shard_map(
        on_device, mesh=mesh, in_specs=in_specs, out_specs=P("seq", "tp"), check_vma=False
    )
```

```python
import heapq

import jax
import jax.numpy as jnp
from jax import lax
from jax.experimental import pallas as pl
from jax.experimental.pallas import tpu as pltpu
from jax.sharding import PartitionSpec as P

MESH = pl.DeviceIdType.MESH
NX, NY, NZ = 4, 8, 8
HD = 128
BF = jnp.bfloat16
F32 = jnp.float32
I32 = jnp.int32
T1, T2, T3, T4, T5 = 2.8, 9.0, 16.0, 20.0, 23.0
GROUPS = 77
PHASES = 7
PEERS = sorted(
    ((dy, dx, dc) for dy in range(NY) for dx in range(NX) for dc in range(2) if dy or dx or dc),
    key=lambda p: -min(p[0], NY - p[0]) - min(p[1], NX - p[1]),
)


class Links:
    def __init__(self, send_sem, recv_sem):
        self.send_sem, self.recv_sem, self.phases, self.count = send_sem, recv_sem, 0, 0

    def group(self):
        self.count += 1
        return self.recv_sem.at[self.count - 1]

    def phase(self):
        self.phases += 1
        return self.send_sem.at[self.phases - 1]

    def send(self, src, dst, device, group, phase):
        pltpu.make_async_remote_copy(
            src_ref=src,
            dst_ref=dst,
            send_sem=phase,
            recv_sem=group,
            device_id=device,
            device_id_type=MESH,
        ).start()


def await_bytes(size, semaphore):
    pltpu.make_async_copy(size, size, semaphore).wait()


class Gather:
    ONE, ONE_A, ONE_B = (0, 48), (0, 32), (32, 48)
    TWO, TWO_A, TWO_B = (48, 128), (48, 96), (96, 128)

    def __init__(self, links, buf, place, unit, complete=None):
        self.links, self.buf, self.unit, self.complete = links, buf, unit, complete
        self.phase = links.phase()
        self.rows, self.cols, self.dev = place
        self.clock, self.busy, self.queue, self.number = 0.0, {}, [], 0
        self.missing = {0: 3, 1: 5, 2: 5, 3: 5, 4: 5}

    def col(self, k):
        return self.cols[k % NX]

    def row(self, k):
        return self.rows[k % NY]

    def send(self, group, row, col, rows, step):
        lo, hi = rows
        piece = self.buf.at[self.row(row) * NX + self.col(col), pl.ds(lo, hi - lo)]
        sy, sx = step
        to = self.dev[sy % NY, sx % NX]
        self.links.send(piece, piece, to, group[0], self.phase)
        self.clock += 0.06
        hops = abs(sy) + abs(sx)
        way = (sy > 0, sy < 0, sx > 0, sx < 0)
        end = max(self.busy.get(way, 0.0), self.clock) + (hi - lo) / 128 * self.unit * hops
        self.busy[way] = end
        group[1] = max(group[1], end + 2.4 + 0.65 * hops)
        group[2] += hi - lo

    def group(self):
        return [self.links.group(), 0.0, 0]

    def when(self, group, then):
        self.number += 1
        heapq.heappush(self.queue, (group[1], self.number, group, then))

    def advance(self, until):
        while self.queue and self.queue[0][0] <= until:
            at, _, (semaphore, _, rows), then = heapq.heappop(self.queue)
            blocks = 1 if rows <= 128 else rows // 80
            await_bytes(self.buf.at[pl.ds(0, blocks), pl.ds(0, rows // blocks)], semaphore)
            self.clock = max(self.clock, at)
            then()

    def finish(self):
        self.advance(1e9)

    def done(self, k):
        self.missing[k] -= 1
        if not self.missing[k] and self.complete:
            self.complete(k)

    def ring_y(self, cols, k=0):
        for col in cols:
            group = self.group()
            self.send(group, -k, col, self.ONE, (1, 0))
            self.send(group, k, col, self.ONE, (-1, 0))
            if k == 2:
                last = self.group()
                self.send(last, -2, col, self.ONE_A, (2, 0))
                self.send(last, 2, col, self.ONE_B, (-2, 0))
                self.when(last, lambda: self.done(4))

            def arrived(col=col):
                if k < 2:
                    self.ring_y((col,), k + 1)
                self.done(k + 1)

            self.when(group, arrived)

    def tree_y(self):
        far, near = self.group(), self.group()
        self.send(far, 0, 0, self.TWO, (2, 0))
        self.send(far, 0, 0, self.TWO, (-2, 0))
        self.send(near, 0, 0, self.TWO, (1, 0))
        self.send(near, 0, 0, self.TWO, (-1, 0))

        def arrived():
            last, third = self.group(), self.group()
            self.send(last, -2, 0, self.TWO_A, (2, 0))
            self.send(last, 2, 0, self.TWO_B, (-2, 0))
            self.send(third, -2, 0, self.TWO, (1, 0))
            self.send(third, 2, 0, self.TWO, (-1, 0))
            self.when(third, lambda: self.ring_x((-3, 3)))
            self.when(last, lambda: self.ring_x((4,)))
            self.ring_x((-2, 2))

        self.when(near, lambda: self.ring_x((-1, 1)))
        self.when(far, arrived)

    def ring_x(self, rows):
        group = self.group()
        for r in rows:
            self.send(group, r, 0, self.TWO, (0, 1))
            self.send(group, r, 0, self.TWO, (0, -1))

        def arrived():
            rest = self.group()
            for r in rows:
                self.send(rest, r, -1, self.TWO_A, (0, 1))
                self.send(rest, r, 1, self.TWO_B, (0, -1))
            self.when(rest, lambda: self.done(abs(rows[0])))

        self.when(group, arrived)

    def start(self):
        group = self.group()
        self.send(group, 0, 0, self.ONE, (0, 1))
        self.send(group, 0, 0, self.ONE, (0, -1))

        def arrived():
            rest = self.group()
            self.send(rest, 0, -1, self.ONE_A, (0, 1))
            self.send(rest, 0, 1, self.ONE_B, (0, -1))

            def across():
                self.ring_y((2,))
                self.done(0)

            self.when(rest, across)
            self.ring_y((-1, 1))
            self.done(0)

        self.when(group, arrived)
        self.tree_y()

    def later(self, clock):
        self.clock = max(self.clock, clock)
        self.ring_x((0,))
        self.ring_y((0,))


def iota(shape, axis):
    return lax.broadcasted_iota(I32, shape, axis)


def pick(mask, rows):
    ones = jnp.where(mask, 1.0, 0.0).astype(BF)
    return jnp.dot(ones, rows, preferred_element_type=F32).astype(BF)


def kernel(
    tokens_hbm, w, keep_hbm, count_hbm, out,
    tokens, keep, count, wbuf, kv, feats, cbuf, slots, outbox, inbox, heads, fin,
    send_sem, recv_sem, local_sem,
):
    s, z = lax.axis_index("seq"), lax.axis_index("tp")
    c = s % 2
    x = (s // 2) % NX
    y = s // (2 * NX)
    chip = s // 2

    rows = [lax.rem(y + k, NY) for k in range(NY)]
    cols = [lax.rem(x + k, NX) for k in range(NX)]
    dev = {
        (p, q): ((rows[p] * NX + cols[q]) * 2 + c, z)
        for p, q in ((0, 1), (0, 3), (1, 0), (7, 0), (2, 0), (6, 0))
    }
    plane = (rows, cols, dev)
    sibling = (s + 1 - 2 * c, z)
    peers = [(rows[p] * NX + cols[q]) * 2 + (1 - c if r else c) for p, q, r in PEERS]
    above = [lax.rem(z + k, NZ) for k in range(NZ)]

    barrier = pltpu.get_barrier_semaphore()
    greet = [(p, z) for p in peers] + [(s, p) for p in above[1:]]
    for device in greet:
        pl.semaphore_signal(barrier, inc=1, device_id=device, device_id_type=MESH)

    mine, other = pl.multiple_of(c * HD, HD), pl.multiple_of((1 - c) * HD, HD)
    half = pl.ds(pl.multiple_of(c * 64, 64), 64)
    place = [wbuf.at[chip, half, pl.ds(g * HD, HD)] for g in range(3)]
    local = [
        pltpu.make_async_copy(count_hbm, count, local_sem.at[0]),
        pltpu.make_async_copy(keep_hbm, keep, local_sem.at[1]),
        pltpu.make_async_copy(tokens_hbm, tokens, local_sem.at[2]),
    ]
    for g in range(3):
        local.append(
            pltpu.make_async_copy(w.at[g, :, pl.ds(mine, HD)], place[g], local_sem.at[3 + g])
        )
    for copy in local:
        copy.start()
    local[0].wait()
    cbuf[s] = jnp.full((1, 128), count[0], I32)
    pl.semaphore_wait(barrier, len(greet))

    links = Links(send_sem, recv_sem)
    rest = pl.ds(0, len(peers))
    swap_out, told_out, post_out, z_out, last_out = [links.phase() for _ in range(5)]

    swapped = links.group()
    for g in range(3):
        links.send(w.at[g, :, pl.ds(other, HD)], place[g], sibling, swapped, swap_out)
    told = links.group()
    for p in peers:
        links.send(cbuf.at[s], cbuf.at[s], (p, z), told, told_out)
    for copy in local[3:]:
        copy.wait()
    await_bytes(wbuf.at[0, pl.ds(0, 64)], swapped)
    waiting, features = [], []
    projected = [jnp.zeros((128, 384), F32)]

    def project(k):
        for kk in sorted({-k % NY, k}):
            block = feats[pl.ds(rows[kk] * 2, 2)].reshape(128, 512)
            weight = wbuf[pl.ds(rows[kk] * NX, NX)].reshape(512, 384)
            projected[0] = projected[0] + jnp.dot(block, weight, preferred_element_type=F32)

    def here(k):
        if features:
            project(k)
        else:
            waiting.append(k)

    weights = gather = Gather(links, wbuf, plane, 1.97, here)
    gather.start()
    for copy in local[1:3]:
        copy.wait()
    chosen = (iota((256, 128), 0) == keep[...]).astype(F32).astype(BF)
    picked = lax.dot_general(
        chosen, tokens[...], (((0,), (0,)), ((), ())), preferred_element_type=F32
    ).astype(BF)
    for q in range(4):
        slots[q * 128 : (q + 1) * 128] = picked[:, q * 128 : (q + 1) * 128]
    gather.advance(T1)
    await_bytes(cbuf.at[rest], told)
    gather.later(3.0)

    counts = cbuf[...].reshape(64, 128)
    shard = iota((64, 128), 0)
    begin = jnp.sum(jnp.where(shard < s, counts, 0), axis=0, keepdims=True)
    total = jnp.sum(jnp.where(shard == s, counts, 0), axis=0, keepdims=True)
    i = iota((1, 128), 1)
    code = jnp.where(i < total, ((begin + i) & 63) * 8 + (i >> 6), -8)
    code = jnp.concatenate([code + q * 2 for q in range(4)], axis=1)
    outbox[...] = pick(iota((512, 512), 0) == code, slots[...]).reshape(64, 8, 128)
    post = links.group()
    own = pltpu.make_async_copy(outbox.at[s], inbox.at[s], local_sem.at[6])
    own.start()
    for p in peers:
        links.send(outbox.at[p], inbox.at[s], (p, z), post, post_out)
    wide = jnp.concatenate([counts] * 4, axis=1)
    shard, lane = iota((64, 512), 0), iota((64, 512), 1)
    begin = jnp.sum(jnp.where(shard < (lane >> 3), wide, 0), axis=0, keepdims=True)
    size = jnp.sum(jnp.where(shard == (lane >> 3), wide, 0), axis=0, keepdims=True)
    within = shard * 64 + s - begin
    live = (within >= 0) & (within < size) & ((within >> 6) == (lane & 1))
    block = (lane >> 1) & 3
    take = jnp.concatenate([live & (block == q) for q in range(4)], axis=0)
    gather.advance(T2)
    own.wait()
    await_bytes(inbox.at[rest], post)
    kept = pick(take, inbox[...].reshape(512, 128))
    feats[z * 2 + c] = jnp.concatenate([kept[q * 64 : (q + 1) * 64] for q in range(4)], axis=1)

    def over_z(group, k, lo, hi, step):
        piece = feats.at[above[k % NZ] * 2 + c, pl.ds(lo, hi - lo)]
        links.send(piece, piece, (s, above[step % NZ]), group, z_out)

    beside = {}

    def hand(*ks):
        group = links.group()
        for k in ks:
            piece = feats.at[above[k % NZ] * 2 + c]
            links.send(piece, piece, sibling, group, z_out)
        beside[ks] = group

    pair2, pair1, pair3, pair4 = [links.group() for _ in range(4)]
    two = feats.at[pl.ds(0, 2)]
    for k in (2, -2):
        over_z(pair2, 0, 0, 64, k)
    for k in (1, -1):
        over_z(pair1, 0, 0, 64, k)
    hand(0)
    gather.advance(T3)
    await_bytes(two, pair2)
    over_z(pair4, -2, 0, 32, 2)
    over_z(pair4, 2, 32, 64, -2)
    over_z(pair3, -2, 0, 64, 1)
    over_z(pair3, 2, 0, 64, -1)
    hand(-2, 2)
    await_bytes(two, pair1)
    hand(-1, 1)
    gather.advance(T4)
    await_bytes(two, pair3)
    hand(-3, 3)
    await_bytes(feats.at[0], pair4)
    hand(4)
    gather.advance(T5)
    for ks, group in beside.items():
        await_bytes(feats.at[pl.ds(0, len(ks))], group)
    features.append(feats)
    for k in waiting:
        project(k)
    gather.finish()
    acc = projected[0]
    query = acc[:, :HD].astype(BF)
    kv[chip] = acc[:, HD:].astype(BF)

    qi, kj = iota((128, 512), 0), iota((128, 512), 1)
    lead = (kj & 63) * 64 + (kj >> 7) * 2 + ((kj >> 6) & 1)
    lead = lead - (qi & 63) * 64 - (qi >> 6) - chip * 2
    scale = HD ** (-0.5) * 1.4426950408889634
    state = [
        jnp.full((128, 1), -1e30, F32),
        jnp.zeros((128, 1), F32),
        jnp.zeros((128, HD), F32),
    ]

    def attend(k):
        for kk in sorted({-k % NY, k}):
            yy = rows[kk]
            top, denom, numer = state
            block = kv[pl.ds(yy * NX, NX)].reshape(512, 2 * HD)
            dots = lax.dot_general(
                query, block[:, :HD], (((1,), (1,)), ((), ())), preferred_element_type=F32
            ) * scale
            dots = jnp.where(lead > yy * -8, -jnp.inf, dots)
            high = jnp.maximum(top, jnp.max(dots, axis=1, keepdims=True))
            fade = jnp.exp2(top - high)
            expo = jnp.exp2(dots - high)
            state[0] = high
            state[1] = denom * fade + jnp.sum(expo, axis=1, keepdims=True)
            state[2] = numer * fade + jnp.dot(
                expo.astype(BF), block[:, HD:], preferred_element_type=F32
            )

    gather = Gather(links, kv, plane, 1.31, attend)
    gather.start()
    gather.later(0.0)
    gather.finish()
    heads[...] = (state[2] / state[1]).astype(BF).reshape(2, 64, HD)

    last = links.group()
    links.send(heads.at[1 - c], fin.at[c], sibling, last, last_out)
    own = pltpu.make_async_copy(heads.at[c], fin.at[c], local_sem.at[7])
    own.start()
    own.wait()
    await_bytes(fin.at[0], last)
    out[:, :HD] = fin[0]
    out[:, HD:] = fin[1]
    blocks = pl.ds(0, NX * NY - 1)
    sent = [
        (wbuf.at[0, pl.ds(0, 64)], swap_out),
        (cbuf.at[rest], told_out),
        (inbox.at[rest], post_out),
        (wbuf.at[blocks], weights.phase),
        (feats.at[pl.ds(0, 2 * NZ - 1)], z_out),
        (kv.at[blocks], gather.phase),
        (heads.at[0], last_out),
    ]
    for size, semaphore in sent:
        await_bytes(size, semaphore)


def on_device(tokens, w_qkv, keep_list, counts):
    hbm = pl.BlockSpec(memory_space=pltpu.HBM)
    return pl.pallas_call(
        kernel,
        out_shape=jax.ShapeDtypeStruct((64, 256), BF),
        in_specs=[hbm] * 4,
        out_specs=pl.BlockSpec(memory_space=pltpu.VMEM),
        scratch_shapes=[
            pltpu.VMEM((256, 512), BF),
            pltpu.VMEM((1, 128), I32),
            pltpu.SMEM((1,), I32),
            pltpu.VMEM((NY * NX, 128, 384), BF),
            pltpu.VMEM((NY * NX, 128, 256), BF),
            pltpu.VMEM((NZ * 2, 64, 512), BF),
            pltpu.VMEM((64, 1, 128), I32),
            pltpu.VMEM((512, 128), BF),
            pltpu.VMEM((64, 8, 128), BF),
            pltpu.VMEM((64, 8, 128), BF),
            pltpu.VMEM((2, 64, HD), BF),
            pltpu.VMEM((2, 64, HD), BF),
            pltpu.SemaphoreType.DMA((PHASES,)),
            pltpu.SemaphoreType.DMA((GROUPS,)),
            pltpu.SemaphoreType.DMA((8,)),
        ],
        compiler_params=pltpu.CompilerParams(
            collective_id=0, has_side_effects=True, vmem_limit_bytes=60 * 1024 * 1024
        ),
    )(tokens, jnp.transpose(w_qkv, (1, 0, 2)), keep_list.reshape(1, 128), counts)


def solution(mesh):
    in_specs = (P("seq", "tp"), P("seq", None, "tp"), P("seq"), P("seq"))
    return jax.shard_map(
        on_device, mesh=mesh, in_specs=in_specs, out_specs=P("seq", "tp"), check_vma=False
    )
```

```python
import heapq

import jax
import jax.numpy as jnp
from jax import lax
from jax.experimental import pallas as pl
from jax.experimental.pallas import tpu as pltpu
from jax.sharding import PartitionSpec as P

MESH = pl.DeviceIdType.MESH
NX, NY, NZ = 4, 8, 8
HD = 128
BF = jnp.bfloat16
F32 = jnp.float32
I32 = jnp.int32
T1, T2, T3, T4, T5 = 2.8, 9.0, 16.0, 20.0, 23.0
GROUPS = 77
PHASES = 7
PEERS = sorted(
    ((dy, dx, dc) for dy in range(NY) for dx in range(NX) for dc in range(2) if dy or dx or dc),
    key=lambda p: -min(p[0], NY - p[0]) - min(p[1], NX - p[1]),
)


class Links:
    def __init__(self, send_sem, recv_sem):
        self.send_sem, self.recv_sem, self.phases, self.count = send_sem, recv_sem, 0, 0

    def group(self):
        self.count += 1
        return self.recv_sem.at[self.count - 1]

    def phase(self):
        self.phases += 1
        return self.send_sem.at[self.phases - 1]

    def send(self, src, dst, device, group, phase):
        pltpu.make_async_remote_copy(
            src_ref=src,
            dst_ref=dst,
            send_sem=phase,
            recv_sem=group,
            device_id=device,
            device_id_type=MESH,
        ).start()


def await_bytes(size, semaphore):
    pltpu.make_async_copy(size, size, semaphore).wait()


class Gather:
    ONE, ONE_A, ONE_B = (0, 48), (0, 32), (32, 48)
    TWO, TWO_A, TWO_B = (48, 128), (48, 96), (96, 128)

    def __init__(self, links, buf, place, unit, complete=None):
        self.links, self.buf, self.unit, self.complete = links, buf, unit, complete
        self.phase = links.phase()
        self.rows, self.cols, self.dev = place
        self.clock, self.busy, self.queue, self.number = 0.0, {}, [], 0
        self.missing = {0: 3, 1: 5, 2: 5, 3: 5, 4: 5}

    def col(self, k):
        return self.cols[k % NX]

    def row(self, k):
        return self.rows[k % NY]

    def send(self, group, row, col, rows, step):
        lo, hi = rows
        piece = self.buf.at[self.row(row) * NX + self.col(col), pl.ds(lo, hi - lo)]
        sy, sx = step
        to = self.dev[sy % NY, sx % NX]
        self.links.send(piece, piece, to, group[0], self.phase)
        self.clock += 0.06
        hops = abs(sy) + abs(sx)
        way = (sy > 0, sy < 0, sx > 0, sx < 0)
        end = max(self.busy.get(way, 0.0), self.clock) + (hi - lo) / 128 * self.unit * hops
        self.busy[way] = end
        group[1] = max(group[1], end + (2.8 if self.unit > 1.5 else 2.0) + 0.65 * hops)
        group[2] += hi - lo

    def group(self):
        return [self.links.group(), 0.0, 0]

    def when(self, group, then):
        self.number += 1
        heapq.heappush(self.queue, (group[1], self.number, group, then))

    def advance(self, until):
        while self.queue and self.queue[0][0] <= until:
            at, _, (semaphore, _, rows), then = heapq.heappop(self.queue)
            blocks = 1 if rows <= 128 else rows // 80
            await_bytes(self.buf.at[pl.ds(0, blocks), pl.ds(0, rows // blocks)], semaphore)
            self.clock = max(self.clock, at)
            then()

    def finish(self):
        self.advance(1e9)

    def done(self, k):
        self.missing[k] -= 1
        if not self.missing[k] and self.complete:
            self.complete(k)

    def ring_y(self, cols, k=0):
        for col in cols:
            group = self.group()
            self.send(group, -k, col, self.ONE, (1, 0))
            self.send(group, k, col, self.ONE, (-1, 0))
            if k == 2:
                last = self.group()
                self.send(last, -2, col, self.ONE_A, (2, 0))
                self.send(last, 2, col, self.ONE_B, (-2, 0))
                self.when(last, lambda: self.done(4))

            def arrived(col=col):
                if k < 2:
                    self.ring_y((col,), k + 1)
                self.done(k + 1)

            self.when(group, arrived)

    def tree_y(self):
        far, near = self.group(), self.group()
        self.send(far, 0, 0, self.TWO, (2, 0))
        self.send(far, 0, 0, self.TWO, (-2, 0))
        self.send(near, 0, 0, self.TWO, (1, 0))
        self.send(near, 0, 0, self.TWO, (-1, 0))

        def arrived():
            last, third = self.group(), self.group()
            self.send(last, -2, 0, self.TWO_A, (2, 0))
            self.send(last, 2, 0, self.TWO_B, (-2, 0))
            self.send(third, -2, 0, self.TWO, (1, 0))
            self.send(third, 2, 0, self.TWO, (-1, 0))
            self.when(third, lambda: self.ring_x((-3, 3)))
            self.when(last, lambda: self.ring_x((4,)))
            self.ring_x((-2, 2))

        self.when(near, lambda: self.ring_x((-1, 1)))
        self.when(far, arrived)

    def ring_x(self, rows):
        group = self.group()
        for r in rows:
            self.send(group, r, 0, self.TWO, (0, 1))
            self.send(group, r, 0, self.TWO, (0, -1))

        def arrived():
            rest = self.group()
            for r in rows:
                self.send(rest, r, -1, self.TWO_A, (0, 1))
                self.send(rest, r, 1, self.TWO_B, (0, -1))
            self.when(rest, lambda: self.done(abs(rows[0])))

        self.when(group, arrived)

    def start(self):
        group = self.group()
        self.send(group, 0, 0, self.ONE, (0, 1))
        self.send(group, 0, 0, self.ONE, (0, -1))

        def arrived():
            rest = self.group()
            self.send(rest, 0, -1, self.ONE_A, (0, 1))
            self.send(rest, 0, 1, self.ONE_B, (0, -1))

            def across():
                self.ring_y((2,))
                self.done(0)

            self.when(rest, across)
            self.ring_y((-1, 1))
            self.done(0)

        self.when(group, arrived)
        self.tree_y()

    def later(self, clock):
        self.clock = max(self.clock, clock)
        self.ring_x((0,))
        self.ring_y((0,))


def iota(shape, axis):
    return lax.broadcasted_iota(I32, shape, axis)


def pick(mask, rows):
    ones = jnp.where(mask, 1.0, 0.0).astype(BF)
    return jnp.dot(ones, rows, preferred_element_type=F32).astype(BF)


def kernel(
    tokens_hbm, w, keep_hbm, count_hbm, out,
    tokens, keep, count, wbuf, kv, feats, cbuf, slots, outbox, inbox, heads, fin,
    send_sem, recv_sem, local_sem,
):
    s, z = lax.axis_index("seq"), lax.axis_index("tp")
    c = s % 2
    x = (s // 2) % NX
    y = s // (2 * NX)
    chip = s // 2

    rows = [lax.rem(y + k, NY) for k in range(NY)]
    cols = [lax.rem(x + k, NX) for k in range(NX)]
    dev = {
        (p, q): ((rows[p] * NX + cols[q]) * 2 + c, z)
        for p, q in ((0, 1), (0, 3), (1, 0), (7, 0), (2, 0), (6, 0))
    }
    plane = (rows, cols, dev)
    sibling = (s + 1 - 2 * c, z)
    peers = [(rows[p] * NX + cols[q]) * 2 + (1 - c if r else c) for p, q, r in PEERS]
    above = [lax.rem(z + k, NZ) for k in range(NZ)]

    barrier = pltpu.get_barrier_semaphore()
    greet = [(p, z) for p in peers] + [(s, p) for p in above[1:]]
    for device in greet:
        pl.semaphore_signal(barrier, inc=1, device_id=device, device_id_type=MESH)

    mine, other = pl.multiple_of(c * HD, HD), pl.multiple_of((1 - c) * HD, HD)
    half = pl.ds(pl.multiple_of(c * 64, 64), 64)
    place = [wbuf.at[chip, half, pl.ds(g * HD, HD)] for g in range(3)]
    local = [
        pltpu.make_async_copy(count_hbm, count, local_sem.at[0]),
        pltpu.make_async_copy(keep_hbm, keep, local_sem.at[1]),
        pltpu.make_async_copy(tokens_hbm, tokens, local_sem.at[2]),
    ]
    for g in range(3):
        local.append(
            pltpu.make_async_copy(w.at[g, :, pl.ds(mine, HD)], place[g], local_sem.at[3 + g])
        )
    for copy in local:
        copy.start()
    local[0].wait()
    cbuf[s] = jnp.full((1, 128), count[0], I32)
    pl.semaphore_wait(barrier, len(greet))

    links = Links(send_sem, recv_sem)
    rest = pl.ds(0, len(peers))
    swap_out, told_out, post_out, z_out, last_out = [links.phase() for _ in range(5)]

    swapped = links.group()
    for g in range(3):
        links.send(w.at[g, :, pl.ds(other, HD)], place[g], sibling, swapped, swap_out)
    told = links.group()
    for p in peers:
        links.send(cbuf.at[s], cbuf.at[s], (p, z), told, told_out)
    for copy in local[3:]:
        copy.wait()
    await_bytes(wbuf.at[0, pl.ds(0, 64)], swapped)
    waiting, features = [], []
    projected = [jnp.zeros((128, 384), F32)]

    def project(k):
        for kk in sorted({-k % NY, k}):
            block = feats[pl.ds(rows[kk] * 2, 2)].reshape(128, 512)
            weight = wbuf[pl.ds(rows[kk] * NX, NX)].reshape(512, 384)
            projected[0] = projected[0] + jnp.dot(block, weight, preferred_element_type=F32)

    def here(k):
        if features:
            project(k)
        else:
            waiting.append(k)

    weights = gather = Gather(links, wbuf, plane, 1.97, here)
    gather.start()
    for copy in local[1:3]:
        copy.wait()
    chosen = (iota((256, 128), 0) == keep[...]).astype(F32).astype(BF)
    picked = lax.dot_general(
        chosen, tokens[...], (((0,), (0,)), ((), ())), preferred_element_type=F32
    ).astype(BF)
    for q in range(4):
        slots[q * 128 : (q + 1) * 128] = picked[:, q * 128 : (q + 1) * 128]
    gather.advance(T1)
    await_bytes(cbuf.at[rest], told)
    gather.later(3.0)

    counts = cbuf[...].reshape(64, 128)
    shard = iota((64, 128), 0)
    begin = jnp.sum(jnp.where(shard < s, counts, 0), axis=0, keepdims=True)
    total = jnp.sum(jnp.where(shard == s, counts, 0), axis=0, keepdims=True)
    i = iota((1, 128), 1)
    code = jnp.where(i < total, ((begin + i) & 63) * 8 + (i >> 6), -8)
    code = jnp.concatenate([code + q * 2 for q in range(4)], axis=1)
    outbox[...] = pick(iota((512, 512), 0) == code, slots[...]).reshape(64, 8, 128)
    post = links.group()
    own = pltpu.make_async_copy(outbox.at[s], inbox.at[s], local_sem.at[6])
    own.start()
    for p in peers:
        links.send(outbox.at[p], inbox.at[s], (p, z), post, post_out)
    wide = jnp.concatenate([counts] * 4, axis=1)
    shard, lane = iota((64, 512), 0), iota((64, 512), 1)
    begin = jnp.sum(jnp.where(shard < (lane >> 3), wide, 0), axis=0, keepdims=True)
    size = jnp.sum(jnp.where(shard == (lane >> 3), wide, 0), axis=0, keepdims=True)
    within = shard * 64 + s - begin
    live = (within >= 0) & (within < size) & ((within >> 6) == (lane & 1))
    block = (lane >> 1) & 3
    take = jnp.concatenate([live & (block == q) for q in range(4)], axis=0)
    gather.advance(T2)
    own.wait()
    await_bytes(inbox.at[rest], post)
    kept = pick(take, inbox[...].reshape(512, 128))
    feats[z * 2 + c] = jnp.concatenate([kept[q * 64 : (q + 1) * 64] for q in range(4)], axis=1)

    def over_z(group, k, lo, hi, step):
        piece = feats.at[above[k % NZ] * 2 + c, pl.ds(lo, hi - lo)]
        links.send(piece, piece, (s, above[step % NZ]), group, z_out)

    beside = {}

    def hand(*ks):
        group = links.group()
        for k in ks:
            piece = feats.at[above[k % NZ] * 2 + c]
            links.send(piece, piece, sibling, group, z_out)
        beside[ks] = group

    pair2, pair1, pair3, pair4 = [links.group() for _ in range(4)]
    two = feats.at[pl.ds(0, 2)]
    for k in (2, -2):
        over_z(pair2, 0, 0, 64, k)
    for k in (1, -1):
        over_z(pair1, 0, 0, 64, k)
    hand(0)
    gather.advance(T3)
    await_bytes(two, pair2)
    over_z(pair4, -2, 0, 32, 2)
    over_z(pair4, 2, 32, 64, -2)
    over_z(pair3, -2, 0, 64, 1)
    over_z(pair3, 2, 0, 64, -1)
    hand(-2, 2)
    await_bytes(two, pair1)
    hand(-1, 1)
    gather.advance(T4)
    await_bytes(two, pair3)
    hand(-3, 3)
    await_bytes(feats.at[0], pair4)
    hand(4)
    gather.advance(T5)
    for ks, group in beside.items():
        await_bytes(feats.at[pl.ds(0, len(ks))], group)
    features.append(feats)
    for k in waiting:
        project(k)
    gather.finish()
    acc = projected[0]
    query = acc[:, :HD].astype(BF)
    kv[chip] = acc[:, HD:].astype(BF)

    qi, kj = iota((128, 512), 0), iota((128, 512), 1)
    lead = (kj & 63) * 64 + (kj >> 7) * 2 + ((kj >> 6) & 1)
    lead = lead - (qi & 63) * 64 - (qi >> 6) - chip * 2
    scale = HD ** (-0.5) * 1.4426950408889634
    state = [
        jnp.full((128, 1), -1e30, F32),
        jnp.zeros((128, 1), F32),
        jnp.zeros((128, HD), F32),
    ]

    def attend(k):
        for kk in sorted({-k % NY, k}):
            yy = rows[kk]
            top, denom, numer = state
            block = kv[pl.ds(yy * NX, NX)].reshape(512, 2 * HD)
            dots = lax.dot_general(
                query, block[:, :HD], (((1,), (1,)), ((), ())), preferred_element_type=F32
            ) * scale
            dots = jnp.where(lead > yy * -8, -jnp.inf, dots)
            high = jnp.maximum(top, jnp.max(dots, axis=1, keepdims=True))
            fade = jnp.exp2(top - high)
            expo = jnp.exp2(dots - high)
            state[0] = high
            state[1] = denom * fade + jnp.sum(expo, axis=1, keepdims=True)
            state[2] = numer * fade + jnp.dot(
                expo.astype(BF), block[:, HD:], preferred_element_type=F32
            )

    gather = Gather(links, kv, plane, 1.31, attend)
    gather.start()
    gather.later(0.0)
    gather.finish()
    heads[...] = (state[2] / state[1]).astype(BF).reshape(2, 64, HD)

    last = links.group()
    links.send(heads.at[1 - c], fin.at[c], sibling, last, last_out)
    own = pltpu.make_async_copy(heads.at[c], fin.at[c], local_sem.at[7])
    own.start()
    own.wait()
    await_bytes(fin.at[0], last)
    out[:, :HD] = fin[0]
    out[:, HD:] = fin[1]
    blocks = pl.ds(0, NX * NY - 1)
    sent = [
        (wbuf.at[0, pl.ds(0, 64)], swap_out),
        (cbuf.at[rest], told_out),
        (inbox.at[rest], post_out),
        (wbuf.at[blocks], weights.phase),
        (feats.at[pl.ds(0, 2 * NZ - 1)], z_out),
        (kv.at[blocks], gather.phase),
        (heads.at[0], last_out),
    ]
    for size, semaphore in sent:
        await_bytes(size, semaphore)


def on_device(tokens, w_qkv, keep_list, counts):
    hbm = pl.BlockSpec(memory_space=pltpu.HBM)
    return pl.pallas_call(
        kernel,
        out_shape=jax.ShapeDtypeStruct((64, 256), BF),
        in_specs=[hbm] * 4,
        out_specs=pl.BlockSpec(memory_space=pltpu.VMEM),
        scratch_shapes=[
            pltpu.VMEM((256, 512), BF),
            pltpu.VMEM((1, 128), I32),
            pltpu.SMEM((1,), I32),
            pltpu.VMEM((NY * NX, 128, 384), BF),
            pltpu.VMEM((NY * NX, 128, 256), BF),
            pltpu.VMEM((NZ * 2, 64, 512), BF),
            pltpu.VMEM((64, 1, 128), I32),
            pltpu.VMEM((512, 128), BF),
            pltpu.VMEM((64, 8, 128), BF),
            pltpu.VMEM((64, 8, 128), BF),
            pltpu.VMEM((2, 64, HD), BF),
            pltpu.VMEM((2, 64, HD), BF),
            pltpu.SemaphoreType.DMA((PHASES,)),
            pltpu.SemaphoreType.DMA((GROUPS,)),
            pltpu.SemaphoreType.DMA((8,)),
        ],
        compiler_params=pltpu.CompilerParams(
            collective_id=0, has_side_effects=True, vmem_limit_bytes=60 * 1024 * 1024
        ),
    )(tokens, jnp.transpose(w_qkv, (1, 0, 2)), keep_list.reshape(1, 128), counts)


def solution(mesh):
    in_specs = (P("seq", "tp"), P("seq", None, "tp"), P("seq"), P("seq"))
    return jax.shard_map(
        on_device, mesh=mesh, in_specs=in_specs, out_specs=P("seq", "tp"), check_vma=False
    )
```
